32 devices in a mesh: seq: 8 (over z, x), mp: 4 (over y, core).
Axes of the slice: x: 2, y: 2, z: 4, core: 2. Of those that a mesh axis runs over, the one named last changes fastest.
Arguments:
- queries: bfloat16 [8192, 1024], P('seq', 'mp'), may hold values from -8 to 8
- byte_keys: bfloat16 [8192, 1024], P('seq', 'mp'), may hold values from -8 to 8
- byte_values: bfloat16 [8192, 1024], P('seq', 'mp'), may hold values from -6 to 6
- w_query: bfloat16 [1024, 1024], P(None, 'mp'), may hold values from -0.1875 to 0.1875
- w_key: bfloat16 [1024, 1024], P(None, 'mp'), may hold values from -0.1875 to 0.1875
- w_value: bfloat16 [1024, 1024], P(None, 'mp'), may hold values from -0.1875 to 0.1875
- w_out: bfloat16 [1024, 1024], P('mp'), may hold values from -0.1875 to 0.1875
- d_output: bfloat16 [8192, 1024], P('seq'), may hold values from -96 to 96
- patch_index: int32 [8192], P('seq'), may hold values from 0 to 2047, as said below
- unpatch: bfloat16 [1024, 4096], P(None, 'mp'), may hold values from -0.09375 to 0.09375
Outputs:
- d_patch: bfloat16 [2048, 4096], P('seq', 'mp')
The draws below stay inside these ranges and needn't reach their ends.
Inputs may be any that keep to these rules, and one draw needn't show every extreme that they name: patch_index never falls and every one of the 2048 patches covers one or more bytes; patch 0 starts at byte 0, and for every k from 1 to 8 - 1 the first byte of patch k * 256 lies 1 to 128 bytes after byte k * 1024, the latter distance reached.
All inputs are finite; a program needn't handle non-finite values.
Results may differ from the reference program's by a relative error of at most 0.025.
Values may be sent and summed in bfloat16 or wider, within the bound.
A program may use at most 128 MiB of HBM per device.

```python
import jax
import jax.numpy as jnp
from jax import lax

D = 1024
G = 4096
HEADS = 16
HS = 64
WINDOW = 512
BYTE_DEV = 1024
PATCH_DEV = 256
TOKENS = 8192
PATCHES = 2048


def draw_queries(key, part):
    key = jax.random.fold_in(key, 11)
    values = jax.random.normal(key, (TOKENS, HEADS * HS), jnp.float32)
    return values.astype(jnp.bfloat16)


def draw_byte_keys(key, part):
    key = jax.random.fold_in(key, 23)
    values = jax.random.normal(key, (TOKENS, HEADS * HS), jnp.float32)
    return values.astype(jnp.bfloat16)


def draw_patch_index(key, part):
    key = jax.random.fold_in(key, 5)
    owners = TOKENS // BYTE_DEV
    reach = BYTE_DEV // 8
    first_key, second_key = jax.random.split(key)
    offsets = jax.random.randint(first_key, (owners + 1,), 1, reach + 1)
    offsets = offsets.at[0].set(0).at[owners].set(0).at[1].set(reach).at[owners - 1].set(reach)
    block_starts = jnp.arange(owners + 1, dtype=jnp.int32) * BYTE_DEV + offsets
    lengths = block_starts[1:] - block_starts[:-1]
    weights = jax.random.randint(second_key, (owners, PATCH_DEV), 1, 17)
    before = jnp.cumsum(weights, axis=1) - weights
    totals = jnp.sum(weights, axis=1, keepdims=True)
    inside = before * (lengths[:, None] - PATCH_DEV) // totals + jnp.arange(PATCH_DEV, dtype=jnp.int32)[None, :]
    starts = (block_starts[:-1, None] + inside).reshape(-1)
    places = jnp.arange(TOKENS, dtype=jnp.int32)
    found = jnp.searchsorted(starts, places, side='right') - 1
    return found.astype(jnp.int32)


def block_scale(rng, dims, shards, smallest, largest):
    level, own = 1.0, jax.random.fold_in(rng, 6)
    for dim, shards_of in shards:
        heights = jnp.exp(jax.random.uniform(jax.random.fold_in(own, dim), (shards_of,), jnp.float32, smallest / len(shards), largest / len(shards)))
        level = level * jnp.repeat(heights, dims[dim] // shards_of).reshape([-1 if axis == dim else 1 for axis in range(len(dims))])
    return level


def bell_draw(rng, shape, scale, limit, cuts=(), kind=jnp.bfloat16):
    values = scale * jax.random.normal(rng, shape, jnp.float32)
    if cuts:
        values = values * block_scale(rng, shape, cuts, -0.22, 0.18)
    return jnp.clip(values, -limit, limit).astype(kind)


def setup_inputs(seed: int = 0) -> dict:
    streams_of = jax.random.split(jax.random.key(seed), 11)
    return {
        "queries": draw_queries(jax.random.fold_in(streams_of[10], 71), 0),
        "byte_keys": draw_byte_keys(jax.random.fold_in(streams_of[10], 71), 0),
        "byte_values": bell_draw(streams_of[2], (TOKENS, HEADS * HS), 1.0, 6.0, ((0, 8), (1, 4))),
        "w_query": bell_draw(streams_of[3], (D, HEADS * HS), D ** -0.5, 0.1875, ((1, 4),)),
        "w_key": bell_draw(streams_of[4], (D, HEADS * HS), D ** -0.5, 0.1875, ((1, 4),)),
        "w_value": bell_draw(streams_of[5], (D, HEADS * HS), D ** -0.5, 0.1875, ((1, 4),)),
        "w_out": bell_draw(streams_of[6], (HEADS * HS, D), (HEADS * HS) ** -0.5, 0.1875, ((0, 4),)),
        "d_output": bell_draw(streams_of[7], (TOKENS, D), 16.0, 96.0, ((0, 8),)),
        "patch_index": draw_patch_index(jax.random.fold_in(streams_of[10], 71), 0),
        "unpatch": bell_draw(streams_of[9], (D, G), G ** -0.5, 0.09375, ((1, 4),)),
    }


def block_grads(query_block, grad_block, key_block, value_block, keep_first):
    block_rows = query_block.shape[0]
    head_count = query_block.shape[1] // HS
    factor = HS ** -0.5
    query_heads = query_block.astype(jnp.float32).reshape(block_rows, head_count, HS)
    grad_heads = grad_block.astype(jnp.float32).reshape(block_rows, head_count, HS)
    key_heads = key_block.astype(jnp.float32).reshape(2 * block_rows, head_count, HS)
    value_heads = value_block.astype(jnp.float32).reshape(2 * block_rows, head_count, HS)
    scores = jnp.einsum("ihd,jhd->hij", query_heads, key_heads) * factor
    query_pos = jnp.arange(block_rows, dtype=jnp.int32)[:, None]
    key_pos = jnp.arange(2 * block_rows, dtype=jnp.int32)[None, :]
    allowed = (key_pos > query_pos) & (key_pos <= query_pos + block_rows) & ((key_pos >= block_rows) | keep_first)
    scores = jnp.where(allowed[None], scores, -1e30)
    peak = jnp.max(scores, axis=-1, keepdims=True)
    raised = jnp.exp(scores - peak)
    attend = raised / jnp.sum(raised, axis=-1, keepdims=True)
    d_attend = jnp.einsum("ihd,jhd->hij", grad_heads, value_heads)
    row_dot = jnp.sum(attend * d_attend, axis=-1, keepdims=True)
    d_scores = (attend * (d_attend - row_dot)).astype(jnp.bfloat16).astype(jnp.float32)
    attend_low = attend.astype(jnp.bfloat16).astype(jnp.float32)
    d_query = jnp.einsum("hij,jhd->ihd", d_scores, key_heads) * factor
    d_key = jnp.einsum("hij,ihd->jhd", d_scores, query_heads) * factor
    d_value = jnp.einsum("hij,ihd->jhd", attend_low, grad_heads)
    return d_query.reshape(block_rows, -1), d_key.reshape(2 * block_rows, -1), d_value.reshape(2 * block_rows, -1)


def spread(parts, width):
    leading = parts[:, :WINDOW].reshape(-1, width)
    trailing = parts[:, WINDOW:].reshape(-1, width)
    blank_rows = jnp.zeros((WINDOW, width), jnp.float32)
    return jnp.concatenate([leading, blank_rows], 0) + jnp.concatenate([blank_rows, trailing], 0)


def reference(queries, byte_keys, byte_values, w_query, w_key, w_value, w_out, d_output, patch_index, unpatch):
    width = queries.shape[1]
    grad_all = jnp.dot(d_output, w_out.T, preferred_element_type=jnp.float32).astype(jnp.bfloat16)
    blank_rows = jnp.zeros((WINDOW, width), byte_keys.dtype)
    padded_keys = jnp.concatenate([blank_rows, byte_keys], 0)
    padded_values = jnp.concatenate([blank_rows, byte_values], 0)

    def one_block(block_id):
        offset = block_id * WINDOW
        return block_grads(lax.dynamic_slice_in_dim(queries, offset, WINDOW, 0),
                           lax.dynamic_slice_in_dim(grad_all, offset, WINDOW, 0),
                           lax.dynamic_slice_in_dim(padded_keys, offset, 2 * WINDOW, 0),
                           lax.dynamic_slice_in_dim(padded_values, offset, 2 * WINDOW, 0),
                           block_id > 0)

    d_query, key_parts, value_parts = lax.map(one_block, jnp.arange(TOKENS // WINDOW, dtype=jnp.int32))
    d_query_low = d_query.reshape(TOKENS, width).astype(jnp.bfloat16)
    d_key_low = spread(key_parts, width)[WINDOW:].astype(jnp.bfloat16)
    d_value_low = spread(value_parts, width)[WINDOW:].astype(jnp.bfloat16)
    byte_grad = (jnp.dot(d_query_low, w_query.T, preferred_element_type=jnp.float32)
                 + jnp.dot(d_key_low, w_key.T, preferred_element_type=jnp.float32)
                 + jnp.dot(d_value_low, w_value.T, preferred_element_type=jnp.float32))
    patch_grad = jax.ops.segment_sum(byte_grad, patch_index, num_segments=PATCHES)
    return jnp.dot(patch_grad.astype(jnp.bfloat16), unpatch, preferred_element_type=jnp.float32).astype(jnp.bfloat16)
```

```python
import functools

import jax
import jax.numpy as jnp
from jax import lax
from jax.experimental import pallas as pl
from jax.experimental.pallas import tpu as pltpu
from jax.sharding import PartitionSpec as P

HS = 64
WINDOW = 512
PATCH_DEV = 256
BLOCK = 256
SPAN = WINDOW + BLOCK
MESH = pl.DeviceIdType.MESH
F32 = jnp.float32
BF16 = jnp.bfloat16


def dot_nt(a, b):
    return lax.dot_general(a, b, (((1,), (1,)), ((), ())), preferred_element_type=F32)


def dot_nn(a, b):
    return lax.dot_general(a, b, (((1,), (0,)), ((), ())), preferred_element_type=F32)


def kernel(
    shards,
    q_hbm,
    k_hbm,
    v_hbm,
    wq_hbm,
    wk_hbm,
    wv_hbm,
    wout_hbm,
    dout_hbm,
    index_ref,
    unpatch_hbm,
    out_ref,
    q,
    kx,
    vx,
    wq,
    wk,
    wv,
    wout,
    dout,
    unpatch,
    dk,
    dv,
    grads,
    p_low,
    ds_low,
    qb,
    gb,
    halo_index,
    prev,
    from_next,
    give,
    take,
    half,
    half_in,
    last,
    total,
    load_sem,
    halo_send,
    halo_recv,
    prev_send,
    prev_recv,
    core_send,
    core_recv,
    far_send,
    far_recv,
    near_send,
    near_recv,
):
    rows = q_hbm.shape[0]
    width = q_hbm.shape[1]
    heads = width // HS
    blocks = rows // BLOCK
    shard = lax.axis_index("seq")
    me = lax.axis_index("mp")
    core = lax.rem(me, 2)
    near = me + 1 - 2 * core
    far = lax.rem(me + 2, 4)
    has_prev = shard > 0
    has_next = shard < shards - 1

    loads = [
        pltpu.make_async_copy(src, dst, load_sem.at[n])
        for n, (src, dst) in enumerate(
            [
                (dout_hbm, dout),
                (wout_hbm, wout),
                (q_hbm, q),
                (k_hbm, kx.at[pl.ds(WINDOW, rows)]),
                (v_hbm, vx.at[pl.ds(WINDOW, rows)]),
                (wq_hbm, wq),
                (wk_hbm, wk),
                (wv_hbm, wv),
                (unpatch_hbm, unpatch),
            ]
        )
    ]
    for load in loads:
        load.start()

    barrier = pltpu.get_barrier_semaphore()
    for mate in (near, far):
        pl.semaphore_signal(barrier, inc=1, device_id=(shard, mate), device_id_type=MESH)

    @pl.when(has_prev)
    def _():
        pl.semaphore_signal(barrier, inc=1, device_id=(shard - 1, me), device_id_type=MESH)

    @pl.when(has_next)
    def _():
        pl.semaphore_signal(barrier, inc=1, device_id=(shard + 1, me), device_id_type=MESH)

    peers = 2 + has_prev.astype(jnp.int32) + has_next.astype(jnp.int32)
    pl.semaphore_wait(barrier, peers)

    def halo(n, src, dst):
        return pltpu.make_async_remote_copy(
            src_ref=src,
            dst_ref=dst,
            send_sem=halo_send.at[n],
            recv_sem=halo_recv.at[n],
            device_id=(shard + 1, me),
            device_id_type=MESH,
        )

    tail = rows - WINDOW
    late = pl.ds(BLOCK, BLOCK)
    early = pl.ds(0, BLOCK)
    halos = [
        halo(0, k_hbm.at[pl.ds(tail + BLOCK, BLOCK)], kx.at[late]),
        halo(1, v_hbm.at[pl.ds(tail + BLOCK, BLOCK)], vx.at[late]),
        halo(2, k_hbm.at[pl.ds(tail, BLOCK)], kx.at[early]),
        halo(3, v_hbm.at[pl.ds(tail, BLOCK)], vx.at[early]),
        halo(4, index_ref, halo_index),
    ]

    @pl.when(has_next)
    def _():
        for copy in halos:
            copy.start()

    @pl.when(shard == 0)
    def _():
        kx[pl.ds(0, WINDOW), :] = jnp.zeros((WINDOW, width), BF16)
        vx[pl.ds(0, WINDOW), :] = jnp.zeros((WINDOW, width), BF16)
        halo_index[...] = jnp.zeros_like(halo_index)

    dk[...] = jnp.zeros_like(dk)
    dv[...] = jnp.zeros_like(dv)
    for load in loads[:5]:
        load.wait()

    def one_hot(index_row, base):
        slot = lax.broadcasted_iota(jnp.int32, (PATCH_DEV, 128), 0)
        return jnp.where(slot == index_row - base, 1.0, 0.0).astype(BF16)

    lane_head = lax.broadcasted_iota(jnp.int32, (BLOCK, width), 1) // HS

    prev_copy = pltpu.make_async_remote_copy(
        src_ref=prev,
        dst_ref=from_next,
        send_sem=prev_send,
        recv_sem=prev_recv,
        device_id=(shard - 1, me),
        device_id_type=MESH,
    )

    def send_prev():
        base = (shard - 1) * PATCH_DEV
        halo_rows = 4
        hot = jnp.concatenate(
            [one_hot(halo_index[pl.ds(4 + c, 1), :], base) for c in range(halo_rows)]
            + [one_hot(index_ref[pl.ds(0, 1), :], base)],
            axis=1,
        )
        span = pl.ds(0, WINDOW + 128)
        prev[:, pl.ds(0, width)] = dot_nn(
            hot[:, WINDOW:], grads[pl.ds(0, 128), pl.ds(0, width)]
        ).astype(BF16)
        prev[:, pl.ds(width, width)] = dot_nn(hot, dk[span, :].astype(BF16)).astype(BF16)
        prev[:, pl.ds(2 * width, width)] = dot_nn(hot, dv[span, :].astype(BF16)).astype(BF16)
        prev_copy.start()

    def one_block(step, carry):
        block = jnp.where(step < 3, 2 - step, 3)
        start = pl.multiple_of(block * BLOCK, BLOCK)

        @pl.when((step == 1) & has_prev)
        def _():
            halos[0].wait_recv()
            halos[1].wait_recv()

        @pl.when((step == 2) & has_prev)
        def _():
            halos[2].wait_recv()
            halos[3].wait_recv()
            halos[4].wait_recv()

        @pl.when((step == 3) & has_prev)
        def _():
            send_prev()

        span = pl.ds(start, SPAN)
        mine = pl.ds(start, BLOCK)
        q_block = (q[mine, :].astype(F32) * HS**-0.5).astype(BF16)
        g_block = dot_nt(dout[mine, :], wout[...]).astype(BF16)
        for h in range(heads):
            keep = lane_head == h
            qb[pl.ds(h * BLOCK, BLOCK), :] = jnp.where(keep, q_block, jnp.zeros_like(q_block))
            gb[pl.ds(h * BLOCK, BLOCK), :] = jnp.where(keep, g_block, jnp.zeros_like(g_block))
        keys = kx[span, :]
        values = vx[span, :]
        keys_t = keys.T
        blocked = jnp.where(shard == 0, jnp.maximum(WINDOW - start, 0), 0)
        key_pos = lax.broadcasted_iota(jnp.int32, (SPAN, BLOCK), 0)
        query_pos = lax.broadcasted_iota(jnp.int32, (SPAN, BLOCK), 1)
        allowed = (key_pos > query_pos) & (key_pos <= query_pos + WINDOW) & (key_pos >= blocked)
        d_query = []
        for h in range(heads):
            head = pl.ds(h * BLOCK, BLOCK)
            scores = jnp.where(allowed, dot_nt(keys, qb[head, :]), -1e30)
            peak = jnp.max(scores, axis=0, keepdims=True)
            raised = jnp.exp(scores - peak)
            d_attend = dot_nt(values, gb[head, :])
            inverse = 1.0 / jnp.sum(raised, axis=0, keepdims=True)
            row_dot = jnp.sum(raised * d_attend, axis=0, keepdims=True) * inverse
            attend = raised * inverse
            d_scores = (attend * (d_attend - row_dot)).astype(BF16)
            p_low[:, head] = attend.astype(BF16)
            ds_low[:, head] = d_scores
            d_query.append(dot_nn(keys_t[h * HS : (h + 1) * HS, :], d_scores))
        dk[span, :] += dot_nn(ds_low[...], qb[...])
        dv[span, :] += dot_nn(p_low[...], gb[...])
        d_query = jnp.concatenate(d_query, axis=0) * HS**-0.5
        grads[mine, pl.ds(0, width)] = d_query.T.astype(BF16)
        return carry

    lax.fori_loop(0, blocks, one_block, 0)

    grads[:, pl.ds(width, width)] = dk[pl.ds(WINDOW, rows), :].astype(BF16)
    grads[:, pl.ds(2 * width, width)] = dv[pl.ds(WINDOW, rows), :].astype(BF16)
    hot = jnp.concatenate(
        [one_hot(index_ref[pl.ds(c, 1), :], shard * PATCH_DEV) for c in range(rows // 128)],
        axis=1,
    )
    pooled = dot_nn(hot, grads[...])
    for load in loads[5:]:
        load.wait()

    total[...] = pooled

    @pl.when(has_next)
    def _():
        prev_copy.wait_recv()
        total[...] += from_next[...].astype(F32)

    def project(first):
        part = total[pl.ds(first, PATCH_DEV // 2), :].astype(BF16)
        return (
            dot_nt(part[:, :width], wq[...])
            + dot_nt(part[:, width : 2 * width], wk[...])
            + dot_nt(part[:, 2 * width :], wv[...])
        )

    side = PATCH_DEV // 2
    give[...] = project(pl.multiple_of((1 - core) * side, side)).astype(BF16)
    core_copy = pltpu.make_async_remote_copy(
        src_ref=give,
        dst_ref=take,
        send_sem=core_send,
        recv_sem=core_recv,
        device_id=(shard, near),
        device_id_type=MESH,
    )
    core_copy.start()
    kept = project(pl.multiple_of(core * side, side))
    core_copy.wait_recv()
    kept = kept + take[...].astype(F32)
    half[...] = kept.astype(BF16)
    far_copy = pltpu.make_async_remote_copy(
        src_ref=half,
        dst_ref=half_in,
        send_sem=far_send,
        recv_sem=far_recv,
        device_id=(shard, far),
        device_id_type=MESH,
    )
    far_copy.start()
    far_copy.wait_recv()
    give_back = (kept + half_in[...].astype(F32)).astype(BF16)
    core_copy.wait_send()
    give[...] = give_back
    near_copy = pltpu.make_async_remote_copy(
        src_ref=give,
        dst_ref=last,
        send_sem=near_send,
        recv_sem=near_recv,
        device_id=(shard, near),
        device_id_type=MESH,
    )
    near_copy.start()
    out_ref[pl.ds(pl.multiple_of(core * side, side), side), :] = dot_nn(
        give[...], unpatch[...]
    ).astype(BF16)
    near_copy.wait_recv()
    out_ref[pl.ds(pl.multiple_of((1 - core) * side, side), side), :] = dot_nn(
        last[...], unpatch[...]
    ).astype(BF16)
    near_copy.wait_send()
    far_copy.wait_send()

    @pl.when(has_prev)
    def _():
        prev_copy.wait_send()

    @pl.when(has_next)
    def _():
        for copy in halos:
            copy.wait_send()


def on_device(
    shards,
    queries,
    byte_keys,
    byte_values,
    w_query,
    w_key,
    w_value,
    w_out,
    d_output,
    patch_index,
    unpatch,
):
    rows, width = queries.shape
    full = w_query.shape[0]
    out_width = unpatch.shape[1]
    heads = width // HS
    side = PATCH_DEV // 2
    vmem = pltpu.VMEM
    dma = pltpu.SemaphoreType.DMA
    anywhere = pl.BlockSpec(memory_space=pl.ANY)
    local = pl.BlockSpec(memory_space=pltpu.VMEM)
    return pl.pallas_call(
        functools.partial(kernel, shards),
        out_shape=jax.ShapeDtypeStruct((PATCH_DEV, out_width), BF16),
        in_specs=[anywhere] * 8 + [local, anywhere],
        out_specs=local,
        scratch_shapes=[
            vmem((rows, width), BF16),
            vmem((rows + WINDOW, width), BF16),
            vmem((rows + WINDOW, width), BF16),
            vmem(w_query.shape, BF16),
            vmem(w_key.shape, BF16),
            vmem(w_value.shape, BF16),
            vmem(w_out.shape, BF16),
            vmem(d_output.shape, BF16),
            vmem(unpatch.shape, BF16),
            vmem((rows + WINDOW, width), F32),
            vmem((rows + WINDOW, width), F32),
            vmem((rows, 3 * width), BF16),
            vmem((SPAN, heads * BLOCK), BF16),
            vmem((SPAN, heads * BLOCK), BF16),
            vmem((heads * BLOCK, width), BF16),
            vmem((heads * BLOCK, width), BF16),
            vmem((8, 128), jnp.int32),
            vmem((PATCH_DEV, 3 * width), BF16),
            vmem((PATCH_DEV, 3 * width), BF16),
            vmem((side, full), BF16),
            vmem((side, full), BF16),
            vmem((side, full), BF16),
            vmem((side, full), BF16),
            vmem((side, full), BF16),
            vmem((PATCH_DEV, 3 * width), F32),
            dma((9,)),
            dma((5,)),
            dma((5,)),
            dma,
            dma,
            dma,
            dma,
            dma,
            dma,
            dma,
            dma,
        ],
        compiler_params=pltpu.CompilerParams(
            collective_id=0, has_side_effects=True, vmem_limit_bytes=56 * 1024 * 1024
        ),
        name="fused_backward",
    )(
        queries,
        byte_keys,
        byte_values,
        w_query,
        w_key,
        w_value,
        w_out,
        d_output,
        patch_index.reshape(8, 128),
        unpatch,
    )


def solution(mesh):
    in_specs = (
        P("seq", "mp"),
        P("seq", "mp"),
        P("seq", "mp"),
        P(None, "mp"),
        P(None, "mp"),
        P(None, "mp"),
        P("mp", None),
        P("seq", None),
        P("seq"),
        P(None, "mp"),
    )
    return jax.shard_map(
        functools.partial(on_device, mesh.shape["seq"]),
        mesh=mesh,
        in_specs=in_specs,
        out_specs=P("seq", "mp"),
        check_vma=False,
    )
```

```python
import functools

import jax
import jax.numpy as jnp
from jax import lax
from jax.experimental import pallas as pl
from jax.experimental.pallas import tpu as pltpu
from jax.sharding import PartitionSpec as P

HS = 64
WINDOW = 512
PATCH_DEV = 256
BLOCK = 256
CHUNK = 128
SPAN = WINDOW + CHUNK
PAIR = 2 * HS
PARTS = 4
MESH = pl.DeviceIdType.MESH
F32 = jnp.float32
BF16 = jnp.bfloat16


def dot_nt(a, b):
    return lax.dot_general(a, b, (((1,), (1,)), ((), ())), preferred_element_type=F32)


def dot_nn(a, b):
    return lax.dot_general(a, b, (((1,), (0,)), ((), ())), preferred_element_type=F32)


def kernel(
    shards,
    q_hbm,
    k_hbm,
    v_hbm,
    wq_hbm,
    wk_hbm,
    wv_hbm,
    wout_hbm,
    dout_hbm,
    index_ref,
    unpatch_hbm,
    out_ref,
    q,
    kx,
    vx,
    wq,
    wk,
    wv,
    wout,
    dout,
    unpatch,
    g,
    dk,
    dv,
    grads,
    halo_index,
    prev,
    from_next,
    give,
    take,
    half,
    half_in,
    done,
    last,
    kept,
    total,
    load_sem,
    halo_send,
    halo_recv,
    prev_send,
    prev_recv,
    core_send,
    core_recv,
    far_send,
    far_recv,
    near_send,
    near_recv,
):
    rows = q_hbm.shape[0]
    width = q_hbm.shape[1]
    pairs = width // PAIR
    shard = lax.axis_index("seq")
    me = lax.axis_index("mp")
    core = lax.rem(me, 2)
    near = me + 1 - 2 * core
    far = lax.rem(me + 2, 4)
    has_prev = shard > 0
    has_next = shard < shards - 1

    def lanes(pair):
        return pl.ds(pair * PAIR, PAIR)

    own = pl.ds(WINDOW, rows)
    moves = [(dout_hbm, dout), (wout_hbm, wout)]
    for pair in range(pairs):
        moves += [
            (q_hbm.at[:, lanes(pair)], q.at[pair]),
            (k_hbm.at[:, lanes(pair)], kx.at[pair, own]),
            (v_hbm.at[:, lanes(pair)], vx.at[pair, own]),
        ]
    soon = len(moves)
    moves += [(wq_hbm, wq), (wk_hbm, wk), (wv_hbm, wv), (unpatch_hbm, unpatch)]
    loads = [
        pltpu.make_async_copy(src, dst, load_sem.at[n]) for n, (src, dst) in enumerate(moves)
    ]
    for load in loads:
        load.start()

    barrier = pltpu.get_barrier_semaphore()
    for mate in (near, far):
        pl.semaphore_signal(barrier, inc=1, device_id=(shard, mate), device_id_type=MESH)

    @pl.when(has_prev)
    def _():
        pl.semaphore_signal(barrier, inc=1, device_id=(shard - 1, me), device_id_type=MESH)

    @pl.when(has_next)
    def _():
        pl.semaphore_signal(barrier, inc=1, device_id=(shard + 1, me), device_id_type=MESH)

    peers = 2 + has_prev.astype(jnp.int32) + has_next.astype(jnp.int32)
    pl.semaphore_wait(barrier, peers)

    def halo(n, src, dst):
        return pltpu.make_async_remote_copy(
            src_ref=src,
            dst_ref=dst,
            send_sem=halo_send.at[n],
            recv_sem=halo_recv.at[n],
            device_id=(shard + 1, me),
            device_id_type=MESH,
        )

    tail = rows - WINDOW
    halos = [halo(0, index_ref, halo_index)]
    for pair in range(pairs):
        for first in (BLOCK, 0):
            for src, dst in ((k_hbm, kx), (v_hbm, vx)):
                halos.append(
                    halo(
                        len(halos),
                        src.at[pl.ds(tail + first, BLOCK), lanes(pair)],
                        dst.at[pair, pl.ds(first, BLOCK)],
                    )
                )

    @pl.when(has_next)
    def _():
        for copy in halos:
            copy.start()

    @pl.when(shard == 0)
    def _():
        kx[:, pl.ds(0, WINDOW), :] = jnp.zeros((pairs, WINDOW, PAIR), BF16)
        vx[:, pl.ds(0, WINDOW), :] = jnp.zeros((pairs, WINDOW, PAIR), BF16)
        halo_index[...] = jnp.zeros_like(halo_index)

    dk[...] = jnp.zeros_like(dk)
    dv[...] = jnp.zeros_like(dv)
    for load in loads[:soon]:
        load.wait()

    def output_grads(block, carry):
        mine = pl.ds(pl.multiple_of(block * BLOCK, BLOCK), BLOCK)
        heads_grad = dot_nt(dout[mine, :], wout[...]).astype(BF16)
        for pair in range(pairs):
            g[pair, mine, :] = heads_grad[:, pair * PAIR : (pair + 1) * PAIR]
        return carry

    lax.fori_loop(0, rows // BLOCK, output_grads, 0)

    def one_hot(index_row, base):
        slot = lax.broadcasted_iota(jnp.int32, (PATCH_DEV, 128), 0)
        return jnp.where(slot == index_row - base, 1.0, 0.0).astype(BF16)

    first_head = lax.broadcasted_iota(jnp.int32, (CHUNK, PAIR), 1) < HS

    def by_head(rows_of):
        blank = jnp.zeros_like(rows_of)
        return jnp.concatenate(
            [jnp.where(first_head, rows_of, blank), jnp.where(first_head, blank, rows_of)], axis=0
        )

    prev_copies = [
        pltpu.make_async_remote_copy(
            src_ref=prev.at[pair],
            dst_ref=from_next.at[pair],
            send_sem=prev_send.at[pair],
            recv_sem=prev_recv.at[pair],
            device_id=(shard - 1, me),
            device_id_type=MESH,
        )
        for pair in range(pairs)
    ]

    def send_prev(pair):
        base = (shard - 1) * PATCH_DEV
        hot = jnp.concatenate(
            [one_hot(halo_index[pl.ds(4 + c, 1), :], base) for c in range(WINDOW // 128)]
            + [one_hot(index_ref[pl.ds(0, 1), :], base)],
            axis=1,
        )
        span = pl.ds(0, WINDOW + 128)
        prev[pair, :, pl.ds(0, PAIR)] = dot_nn(
            hot[:, WINDOW:], grads[pl.ds(0, 128), lanes(pair)]
        ).astype(BF16)
        terms = jnp.concatenate([dk[pair, span, :], dv[pair, span, :]], axis=1).astype(BF16)
        prev[pair, :, pl.ds(PAIR, 2 * PAIR)] = dot_nn(hot, terms).astype(BF16)
        prev_copies[pair].start()

    top_key = lax.broadcasted_iota(jnp.int32, (CHUNK, 2 * CHUNK), 0)
    query_pos = lax.rem(lax.broadcasted_iota(jnp.int32, (CHUNK, 2 * CHUNK), 1), CHUNK)
    middle_key = lax.broadcasted_iota(jnp.int32, (WINDOW - CHUNK, 2 * CHUNK), 0) + CHUNK

    def one_step(step, carry):
        block = jnp.where(step < 2, 2, jnp.where(step < 6, 1 - lax.rem(step, 2), 3))
        pair = jnp.where((step >= 2) & (step < 6), (step - 2) // 2, lax.rem(step, 2))

        for n in range(4):

            @pl.when((step == 2 + n) & has_prev)
            def _(n=n):
                if n == 0:
                    halos[0].wait_recv()
                halos[1 + 2 * n].wait_recv()
                halos[2 + 2 * n].wait_recv()

        for n in range(pairs):

            @pl.when((step == 4 + 2 * n) & has_prev)
            def _(n=n):
                send_prev(n)

        column = pl.ds(pl.multiple_of(pair * PAIR, PAIR), PAIR)
        results = []
        for c in range(BLOCK // CHUNK):
            start = pl.multiple_of(block * BLOCK + c * CHUNK, CHUNK)
            span = pl.ds(start, SPAN)
            mine = pl.ds(start, CHUNK)
            queries = by_head((q[pair, mine, :].astype(F32) * HS**-0.5).astype(BF16))
            grads_in = by_head(g[pair, mine, :])
            keys = kx[pair, span, :]
            values = vx[pair, span, :]
            blocked = jnp.where(shard == 0, jnp.maximum(WINDOW - start, 0), 0)
            scores = dot_nt(keys, queries)
            scores = jnp.concatenate(
                [
                    jnp.where(
                        top_key > jnp.maximum(query_pos, blocked - 1), scores[:CHUNK], -1e30
                    ),
                    jnp.where(middle_key >= blocked, scores[CHUNK:WINDOW], -1e30),
                    jnp.where(top_key <= query_pos, scores[WINDOW:], -1e30),
                ],
                axis=0,
            )
            peak = jnp.max(scores, axis=0, keepdims=True)
            raised = jnp.exp(scores - peak)
            d_attend = dot_nt(values, grads_in)
            inverse = 1.0 / jnp.sum(raised, axis=0, keepdims=True)
            row_dot = jnp.sum(raised * d_attend, axis=0, keepdims=True) * inverse
            attend = raised * inverse
            d_scores = (attend * (d_attend - row_dot)).astype(BF16)
            d_query = dot_nn(keys.T, d_scores) * HS**-0.5
            d_query = jnp.concatenate([d_query[:HS, :CHUNK], d_query[HS:, CHUNK:]], axis=0)
            results.append(
                (
                    span,
                    mine,
                    d_query.T.astype(BF16),
                    dot_nn(d_scores, queries),
                    dot_nn(attend.astype(BF16), grads_in),
                )
            )
        for span, mine, d_query, d_key, d_value in results:
            grads[mine, column] = d_query
            dk[pair, span, :] += d_key
            dv[pair, span, :] += d_value
        return carry

    lax.fori_loop(0, rows // BLOCK * pairs, one_step, 0)

    for pair in range(pairs):
        grads[:, pl.ds(width + pair * PAIR, PAIR)] = dk[pair, own, :].astype(BF16)
        grads[:, pl.ds(2 * width + pair * PAIR, PAIR)] = dv[pair, own, :].astype(BF16)
    hot = jnp.concatenate(
        [one_hot(index_ref[pl.ds(c, 1), :], shard * PATCH_DEV) for c in range(rows // 128)],
        axis=1,
    )
    pooled = dot_nn(hot, grads[...])
    for load in loads[soon:]:
        load.wait()

    total[...] = pooled

    @pl.when(has_next)
    def _():
        for pair in range(pairs):
            prev_copies[pair].wait_recv()
            for n in range(3):
                total[:, pl.ds(n * width + pair * PAIR, PAIR)] += from_next[
                    pair, :, pl.ds(n * PAIR, PAIR)
                ].astype(F32)

    def project(first):
        part = total[pl.ds(first, PATCH_DEV // 2), :].astype(BF16)
        return (
            dot_nt(part[:, :width], wq[...])
            + dot_nt(part[:, width : 2 * width], wk[...])
            + dot_nt(part[:, 2 * width :], wv[...])
        )

    side = PATCH_DEV // 2
    part = side // PARTS

    def swap(src, dst, sends, recvs, mate):
        return [
            pltpu.make_async_remote_copy(
                src_ref=src.at[pl.ds(n * part, part)],
                dst_ref=dst.at[pl.ds(n * part, part)],
                send_sem=sends.at[n],
                recv_sem=recvs.at[n],
                device_id=(shard, mate),
                device_id_type=MESH,
            )
            for n in range(PARTS)
        ]

    core_copies = swap(give, take, core_send, core_recv, near)
    far_copies = swap(half, half_in, far_send, far_recv, far)
    near_copies = swap(done, last, near_send, near_recv, near)
    give[...] = project(pl.multiple_of((1 - core) * side, side)).astype(BF16)
    for copy in core_copies:
        copy.start()
    kept[...] = project(pl.multiple_of(core * side, side))
    for n in range(PARTS):
        piece = pl.ds(n * part, part)
        core_copies[n].wait_recv()
        kept[piece, :] += take[piece, :].astype(F32)
        half[piece, :] = kept[piece, :].astype(BF16)
        far_copies[n].start()
    for n in range(PARTS):
        piece = pl.ds(n * part, part)
        far_copies[n].wait_recv()
        done[piece, :] = (kept[piece, :] + half_in[piece, :].astype(F32)).astype(BF16)
        near_copies[n].start()
    out_ref[pl.ds(pl.multiple_of(core * side, side), side), :] = dot_nn(
        done[...], unpatch[...]
    ).astype(BF16)
    for copy in near_copies:
        copy.wait_recv()
    out_ref[pl.ds(pl.multiple_of((1 - core) * side, side), side), :] = dot_nn(
        last[...], unpatch[...]
    ).astype(BF16)
    for copy in core_copies + far_copies + near_copies:
        copy.wait_send()

    @pl.when(has_prev)
    def _():
        for copy in prev_copies:
            copy.wait_send()

    @pl.when(has_next)
    def _():
        for copy in halos:
            copy.wait_send()


def on_device(
    shards,
    queries,
    byte_keys,
    byte_values,
    w_query,
    w_key,
    w_value,
    w_out,
    d_output,
    patch_index,
    unpatch,
):
    rows, width = queries.shape
    full = w_query.shape[0]
    out_width = unpatch.shape[1]
    pairs = width // PAIR
    side = PATCH_DEV // 2
    vmem = pltpu.VMEM
    dma = pltpu.SemaphoreType.DMA
    anywhere = pl.BlockSpec(memory_space=pl.ANY)
    local = pl.BlockSpec(memory_space=pltpu.VMEM)
    return pl.pallas_call(
        functools.partial(kernel, shards),
        out_shape=jax.ShapeDtypeStruct((PATCH_DEV, out_width), BF16),
        in_specs=[anywhere] * 8 + [local, anywhere],
        out_specs=local,
        scratch_shapes=[
            vmem((pairs, rows, PAIR), BF16),
            vmem((pairs, rows + WINDOW, PAIR), BF16),
            vmem((pairs, rows + WINDOW, PAIR), BF16),
            vmem(w_query.shape, BF16),
            vmem(w_key.shape, BF16),
            vmem(w_value.shape, BF16),
            vmem(w_out.shape, BF16),
            vmem(d_output.shape, BF16),
            vmem(unpatch.shape, BF16),
            vmem((pairs, rows, PAIR), BF16),
            vmem((pairs, rows + WINDOW, PAIR), F32),
            vmem((pairs, rows + WINDOW, PAIR), F32),
            vmem((rows, 3 * width), BF16),
            vmem((8, 128), jnp.int32),
            vmem((pairs, PATCH_DEV, 3 * PAIR), BF16),
            vmem((pairs, PATCH_DEV, 3 * PAIR), BF16),
            vmem((side, full), BF16),
            vmem((side, full), BF16),
            vmem((side, full), BF16),
            vmem((side, full), BF16),
            vmem((side, full), BF16),
            vmem((side, full), BF16),
            vmem((side, full), F32),
            vmem((PATCH_DEV, 3 * width), F32),
            dma((6 + 3 * pairs,)),
            dma((1 + 4 * pairs,)),
            dma((1 + 4 * pairs,)),
            dma((pairs,)),
            dma((pairs,)),
            dma((PARTS,)),
            dma((PARTS,)),
            dma((PARTS,)),
            dma((PARTS,)),
            dma((PARTS,)),
            dma((PARTS,)),
        ],
        compiler_params=pltpu.CompilerParams(
            collective_id=0, has_side_effects=True, vmem_limit_bytes=56 * 1024 * 1024
        ),
        name="fused_backward",
    )(
        queries,
        byte_keys,
        byte_values,
        w_query,
        w_key,
        w_value,
        w_out,
        d_output,
        patch_index.reshape(8, 128),
        unpatch,
    )


def solution(mesh):
    in_specs = (
        P("seq", "mp"),
        P("seq", "mp"),
        P("seq", "mp"),
        P(None, "mp"),
        P(None, "mp"),
        P(None, "mp"),
        P("mp", None),
        P("seq", None),
        P("seq"),
        P(None, "mp"),
    )
    return jax.shard_map(
        functools.partial(on_device, mesh.shape["seq"]),
        mesh=mesh,
        in_specs=in_specs,
        out_specs=P("seq", "mp"),
        check_vma=False,
    )
```

```python
import functools

import jax
import jax.numpy as jnp
from jax import lax
from jax.experimental import pallas as pl
from jax.experimental.pallas import tpu as pltpu
from jax.sharding import PartitionSpec as P

HS = 64
WINDOW = 512
PATCH_DEV = 256
BLOCK = 256
CHUNK = 128
SPAN = WINDOW + CHUNK
PAIR = 2 * HS
PARTS = 4
MESH = pl.DeviceIdType.MESH
F32 = jnp.float32
BF16 = jnp.bfloat16


def dot_nt(a, b):
    return lax.dot_general(a, b, (((1,), (1,)), ((), ())), preferred_element_type=F32)


def dot_nn(a, b):
    return lax.dot_general(a, b, (((1,), (0,)), ((), ())), preferred_element_type=F32)


def kernel(
    shards,
    q_hbm,
    k_hbm,
    v_hbm,
    wq_hbm,
    wk_hbm,
    wv_hbm,
    wout_hbm,
    dout_hbm,
    index_ref,
    unpatch_hbm,
    out_ref,
    q,
    kx,
    vx,
    wq,
    wk,
    wv,
    wout,
    dout,
    unpatch,
    g,
    dk,
    dv,
    grads,
    halo_index,
    prev,
    from_next,
    give,
    take,
    half,
    half_in,
    done,
    last,
    kept,
    total,
    load_sem,
    halo_send,
    halo_recv,
    prev_send,
    prev_recv,
    core_send,
    core_recv,
    far_send,
    far_recv,
    near_send,
    near_recv,
):
    rows = q_hbm.shape[0]
    width = q_hbm.shape[1]
    pairs = width // PAIR
    shard = lax.axis_index("seq")
    me = lax.axis_index("mp")
    core = lax.rem(me, 2)
    near = me + 1 - 2 * core
    far = lax.rem(me + 2, 4)
    has_prev = shard > 0
    has_next = shard < shards - 1

    def lanes(pair):
        return pl.ds(pair * PAIR, PAIR)

    own = pl.ds(WINDOW, rows)
    moves = [(dout_hbm, dout), (wout_hbm, wout)]
    for pair in range(pairs):
        moves += [
            (q_hbm.at[:, lanes(pair)], q.at[pair]),
            (k_hbm.at[:, lanes(pair)], kx.at[pair, own]),
            (v_hbm.at[:, lanes(pair)], vx.at[pair, own]),
        ]
    soon = len(moves)
    moves += [(wq_hbm, wq), (wk_hbm, wk), (wv_hbm, wv), (unpatch_hbm, unpatch)]
    loads = [
        pltpu.make_async_copy(src, dst, load_sem.at[n]) for n, (src, dst) in enumerate(moves)
    ]
    for load in loads:
        load.start()

    barrier = pltpu.get_barrier_semaphore()
    for mate in (near, far):
        pl.semaphore_signal(barrier, inc=1, device_id=(shard, mate), device_id_type=MESH)

    @pl.when(has_prev)
    def _():
        pl.semaphore_signal(barrier, inc=1, device_id=(shard - 1, me), device_id_type=MESH)

    @pl.when(has_next)
    def _():
        pl.semaphore_signal(barrier, inc=1, device_id=(shard + 1, me), device_id_type=MESH)

    peers = 2 + has_prev.astype(jnp.int32) + has_next.astype(jnp.int32)
    pl.semaphore_wait(barrier, peers)

    def halo(n, src, dst):
        return pltpu.make_async_remote_copy(
            src_ref=src,
            dst_ref=dst,
            send_sem=halo_send.at[n],
            recv_sem=halo_recv.at[n],
            device_id=(shard + 1, me),
            device_id_type=MESH,
        )

    tail = rows - WINDOW
    halos = [halo(0, index_ref, halo_index)]
    for pair in range(pairs):
        for first in (BLOCK, 0):
            for src, dst in ((k_hbm, kx), (v_hbm, vx)):
                halos.append(
                    halo(
                        len(halos),
                        src.at[pl.ds(tail + first, BLOCK), lanes(pair)],
                        dst.at[pair, pl.ds(first, BLOCK)],
                    )
                )

    @pl.when(has_next)
    def _():
        for copy in halos:
            copy.start()

    @pl.when(shard == 0)
    def _():
        kx[:, pl.ds(0, WINDOW), :] = jnp.zeros((pairs, WINDOW, PAIR), BF16)
        vx[:, pl.ds(0, WINDOW), :] = jnp.zeros((pairs, WINDOW, PAIR), BF16)
        halo_index[...] = jnp.zeros_like(halo_index)

    dk[...] = jnp.zeros_like(dk)
    dv[...] = jnp.zeros_like(dv)
    for load in loads[:soon]:
        load.wait()

    def output_grads(block, carry):
        mine = pl.ds(pl.multiple_of(block * BLOCK, BLOCK), BLOCK)
        heads_grad = dot_nt(dout[mine, :], wout[...]).astype(BF16)
        for pair in range(pairs):
            g[pair, mine, :] = heads_grad[:, pair * PAIR : (pair + 1) * PAIR]
        return carry

    lax.fori_loop(0, rows // BLOCK, output_grads, 0)

    def one_hot(index_row, base):
        slot = lax.broadcasted_iota(jnp.int32, (PATCH_DEV, 128), 0)
        return jnp.where(slot == index_row - base, 1.0, 0.0).astype(BF16)

    first_head = lax.broadcasted_iota(jnp.int32, (CHUNK, PAIR), 1) < HS

    def by_head(rows_of):
        blank = jnp.zeros_like(rows_of)
        return jnp.concatenate(
            [jnp.where(first_head, rows_of, blank), jnp.where(first_head, blank, rows_of)], axis=0
        )

    prev_copies = [
        pltpu.make_async_remote_copy(
            src_ref=prev.at[pair],
            dst_ref=from_next.at[pair],
            send_sem=prev_send.at[pair],
            recv_sem=prev_recv.at[pair],
            device_id=(shard - 1, me),
            device_id_type=MESH,
        )
        for pair in range(pairs)
    ]

    def send_prev(pair):
        base = (shard - 1) * PATCH_DEV
        hot = jnp.concatenate(
            [one_hot(halo_index[pl.ds(4 + c, 1), :], base) for c in range(WINDOW // 128)]
            + [one_hot(index_ref[pl.ds(0, 1), :], base)],
            axis=1,
        )
        span = pl.ds(0, WINDOW + 128)
        prev[pair, :, pl.ds(0, PAIR)] = dot_nn(
            hot[:, WINDOW:], grads[pl.ds(0, 128), lanes(pair)]
        ).astype(BF16)
        terms = jnp.concatenate([dk[pair, span, :], dv[pair, span, :]], axis=1).astype(BF16)
        prev[pair, :, pl.ds(PAIR, 2 * PAIR)] = dot_nn(hot, terms).astype(BF16)
        prev_copies[pair].start()

    top_key = lax.broadcasted_iota(jnp.int32, (CHUNK, 2 * CHUNK), 0)
    query_pos = lax.rem(lax.broadcasted_iota(jnp.int32, (CHUNK, 2 * CHUNK), 1), CHUNK)
    middle_key = lax.broadcasted_iota(jnp.int32, (WINDOW - CHUNK, 2 * CHUNK), 0) + CHUNK

    def column(row):
        return jnp.broadcast_to(row, (PAIR, CHUNK)).T

    def one_step(step, carry):
        for n in range(pairs):

            @pl.when((step == 1 + n) & has_prev)
            def _(n=n):
                if n == 0:
                    halos[0].wait_recv()
                for copy in halos[1 + 4 * n : 5 + 4 * n]:
                    copy.wait_recv()

            @pl.when((step == 2 + n) & has_prev)
            def _(n=n):
                send_prev(n)

        outer = (step == 0) | (step == 3)
        chains = []
        for n in range(2):
            block = jnp.where(step == 0, 2, jnp.where(step == 3, 3, 1 - n))
            pair = jnp.where(outer, n, step - 1)
            chains += [(block, pair, c) for c in range(BLOCK // CHUNK)]
        results = []
        for block, pair, c in chains:
            start = pl.multiple_of(block * BLOCK + c * CHUNK, CHUNK)
            span = pl.ds(start, SPAN)
            mine = pl.ds(start, CHUNK)
            queries = by_head((q[pair, mine, :].astype(F32) * HS**-0.5).astype(BF16))
            keys = kx[pair, span, :]
            values = vx[pair, span, :]
            blocked = jnp.where(shard == 0, jnp.maximum(WINDOW - start, 0), 0)
            scores = dot_nt(keys, queries)
            scores = jnp.concatenate(
                [
                    jnp.where(
                        top_key > jnp.maximum(query_pos, blocked - 1), scores[:CHUNK], -1e30
                    ),
                    jnp.where(middle_key >= blocked, scores[CHUNK:WINDOW], -1e30),
                    jnp.where(top_key <= query_pos, scores[WINDOW:], -1e30),
                ],
                axis=0,
            )
            peak = jnp.max(scores, axis=0, keepdims=True)
            raised = jnp.exp(scores - peak)
            inverse = 1.0 / jnp.sum(raised, axis=0, keepdims=True)
            scale = jnp.where(
                first_head, column(inverse[:, :CHUNK]), column(inverse[:, CHUNK:])
            )
            grads_in = by_head((g[pair, mine, :].astype(F32) * scale).astype(BF16))
            d_attend = dot_nt(values, grads_in)
            row_dot = jnp.sum(raised * d_attend, axis=0, keepdims=True) * inverse
            d_scores = (raised * (d_attend - row_dot)).astype(BF16)
            d_query = dot_nn(keys.T, d_scores) * HS**-0.5
            d_query = jnp.concatenate([d_query[:HS, :CHUNK], d_query[HS:, CHUNK:]], axis=0)
            results.append(
                (
                    pair,
                    span,
                    mine,
                    d_query.T.astype(BF16),
                    dot_nn(d_scores, queries),
                    dot_nn(raised.astype(BF16), grads_in),
                )
            )
        for pair, span, mine, d_query, d_key, d_value in results:
            grads[mine, pl.ds(pl.multiple_of(pair * PAIR, PAIR), PAIR)] = d_query
            dk[pair, span, :] += d_key
            dv[pair, span, :] += d_value
        return carry

    lax.fori_loop(0, rows // BLOCK, one_step, 0)

    for pair in range(pairs):
        grads[:, pl.ds(width + pair * PAIR, PAIR)] = dk[pair, own, :].astype(BF16)
        grads[:, pl.ds(2 * width + pair * PAIR, PAIR)] = dv[pair, own, :].astype(BF16)
    hot = jnp.concatenate(
        [one_hot(index_ref[pl.ds(c, 1), :], shard * PATCH_DEV) for c in range(rows // 128)],
        axis=1,
    )
    pooled = dot_nn(hot, grads[...])
    for load in loads[soon:]:
        load.wait()

    total[...] = pooled

    @pl.when(has_next)
    def _():
        for pair in range(pairs):
            prev_copies[pair].wait_recv()
            for n in range(3):
                total[:, pl.ds(n * width + pair * PAIR, PAIR)] += from_next[
                    pair, :, pl.ds(n * PAIR, PAIR)
                ].astype(F32)

    def project(first):
        part = total[pl.ds(first, PATCH_DEV // 2), :].astype(BF16)
        return (
            dot_nt(part[:, :width], wq[...])
            + dot_nt(part[:, width : 2 * width], wk[...])
            + dot_nt(part[:, 2 * width :], wv[...])
        )

    side = PATCH_DEV // 2
    part = side // PARTS

    def swap(src, dst, sends, recvs, mate):
        return [
            pltpu.make_async_remote_copy(
                src_ref=src.at[pl.ds(n * part, part)],
                dst_ref=dst.at[pl.ds(n * part, part)],
                send_sem=sends.at[n],
                recv_sem=recvs.at[n],
                device_id=(shard, mate),
                device_id_type=MESH,
            )
            for n in range(PARTS)
        ]

    core_copies = swap(give, take, core_send, core_recv, near)
    far_copies = swap(half, half_in, far_send, far_recv, far)
    near_copies = swap(done, last, near_send, near_recv, near)
    give[...] = project(pl.multiple_of((1 - core) * side, side)).astype(BF16)
    for copy in core_copies:
        copy.start()
    kept[...] = project(pl.multiple_of(core * side, side))
    for n in range(PARTS):
        piece = pl.ds(n * part, part)
        core_copies[n].wait_recv()
        kept[piece, :] += take[piece, :].astype(F32)
        half[piece, :] = kept[piece, :].astype(BF16)
        far_copies[n].start()
    for n in range(PARTS):
        piece = pl.ds(n * part, part)
        far_copies[n].wait_recv()
        done[piece, :] = (kept[piece, :] + half_in[piece, :].astype(F32)).astype(BF16)
        near_copies[n].start()
    out_ref[pl.ds(pl.multiple_of(core * side, side), side), :] = dot_nn(
        done[...], unpatch[...]
    ).astype(BF16)
    for copy in near_copies:
        copy.wait_recv()
    out_ref[pl.ds(pl.multiple_of((1 - core) * side, side), side), :] = dot_nn(
        last[...], unpatch[...]
    ).astype(BF16)
    for copy in core_copies + far_copies + near_copies:
        copy.wait_send()

    @pl.when(has_prev)
    def _():
        for copy in prev_copies:
            copy.wait_send()

    @pl.when(has_next)
    def _():
        for copy in halos:
            copy.wait_send()


def on_device(
    shards,
    queries,
    byte_keys,
    byte_values,
    w_query,
    w_key,
    w_value,
    w_out,
    d_output,
    patch_index,
    unpatch,
):
    rows, width = queries.shape
    full = w_query.shape[0]
    out_width = unpatch.shape[1]
    pairs = width // PAIR
    side = PATCH_DEV // 2
    vmem = pltpu.VMEM
    dma = pltpu.SemaphoreType.DMA
    anywhere = pl.BlockSpec(memory_space=pl.ANY)
    local = pl.BlockSpec(memory_space=pltpu.VMEM)
    return pl.pallas_call(
        functools.partial(kernel, shards),
        out_shape=jax.ShapeDtypeStruct((PATCH_DEV, out_width), BF16),
        in_specs=[anywhere] * 8 + [local, anywhere],
        out_specs=local,
        scratch_shapes=[
            vmem((pairs, rows, PAIR), BF16),
            vmem((pairs, rows + WINDOW, PAIR), BF16),
            vmem((pairs, rows + WINDOW, PAIR), BF16),
            vmem(w_query.shape, BF16),
            vmem(w_key.shape, BF16),
            vmem(w_value.shape, BF16),
            vmem(w_out.shape, BF16),
            vmem(d_output.shape, BF16),
            vmem(unpatch.shape, BF16),
            vmem((pairs, rows, PAIR), BF16),
            vmem((pairs, rows + WINDOW, PAIR), F32),
            vmem((pairs, rows + WINDOW, PAIR), F32),
            vmem((rows, 3 * width), BF16),
            vmem((8, 128), jnp.int32),
            vmem((pairs, PATCH_DEV, 3 * PAIR), BF16),
            vmem((pairs, PATCH_DEV, 3 * PAIR), BF16),
            vmem((side, full), BF16),
            vmem((side, full), BF16),
            vmem((side, full), BF16),
            vmem((side, full), BF16),
            vmem((side, full), BF16),
            vmem((side, full), BF16),
            vmem((side, full), F32),
            vmem((PATCH_DEV, 3 * width), F32),
            dma((6 + 3 * pairs,)),
            dma((1 + 4 * pairs,)),
            dma((1 + 4 * pairs,)),
            dma((pairs,)),
            dma((pairs,)),
            dma((PARTS,)),
            dma((PARTS,)),
            dma((PARTS,)),
            dma((PARTS,)),
            dma((PARTS,)),
            dma((PARTS,)),
        ],
        compiler_params=pltpu.CompilerParams(
            collective_id=0, has_side_effects=True, vmem_limit_bytes=56 * 1024 * 1024
        ),
        name="fused_backward",
    )(
        queries,
        byte_keys,
        byte_values,
        w_query,
        w_key,
        w_value,
        w_out,
        d_output,
        patch_index.reshape(8, 128),
        unpatch,
    )


def solution(mesh):
    in_specs = (
        P("seq", "mp"),
        P("seq", "mp"),
        P("seq", "mp"),
        P(None, "mp"),
        P(None, "mp"),
        P(None, "mp"),
        P("mp", None),
        P("seq", None),
        P("seq"),
        P(None, "mp"),
    )
    return jax.shard_map(
        functools.partial(on_device, mesh.shape["seq"]),
        mesh=mesh,
        in_specs=in_specs,
        out_specs=P("seq", "mp"),
        check_vma=False,
    )
```

```python
import functools

import jax
import jax.numpy as jnp
from jax import lax
from jax.experimental import pallas as pl
from jax.experimental.pallas import tpu as pltpu
from jax.sharding import PartitionSpec as P

HS = 64
WINDOW = 512
PATCH_DEV = 256
BLOCK = 256
CHUNK = 128
SPAN = WINDOW + CHUNK
PAIR = 2 * HS
PARTS = 4
PIECES = SPAN // CHUNK
MESH = pl.DeviceIdType.MESH
F32 = jnp.float32
BF16 = jnp.bfloat16


def dot_nt(a, b):
    return lax.dot_general(a, b, (((1,), (1,)), ((), ())), preferred_element_type=F32)


def dot_nn(a, b):
    return lax.dot_general(a, b, (((1,), (0,)), ((), ())), preferred_element_type=F32)


def kernel(
    shards,
    q_hbm,
    k_hbm,
    v_hbm,
    wq_hbm,
    wk_hbm,
    wv_hbm,
    wout_hbm,
    dout_hbm,
    index_ref,
    unpatch_hbm,
    out_ref,
    q,
    kx,
    vx,
    wq,
    wk,
    wv,
    wout,
    dout,
    unpatch,
    g,
    dk,
    dv,
    grads,
    scores,
    d_attend,
    p_low,
    ds_low,
    halo_index,
    prev,
    from_next,
    give,
    take,
    half,
    half_in,
    done,
    last,
    kept,
    total,
    load_sem,
    halo_send,
    halo_recv,
    prev_send,
    prev_recv,
    core_send,
    core_recv,
    far_send,
    far_recv,
    near_send,
    near_recv,
):
    rows = q_hbm.shape[0]
    width = q_hbm.shape[1]
    pairs = width // PAIR
    shard = lax.axis_index("seq")
    me = lax.axis_index("mp")
    core = lax.rem(me, 2)
    near = me + 1 - 2 * core
    far = lax.rem(me + 2, 4)
    has_prev = shard > 0
    has_next = shard < shards - 1

    def lanes(pair):
        return pl.ds(pair * PAIR, PAIR)

    own = pl.ds(WINDOW, rows)
    moves = [(dout_hbm, dout), (wout_hbm, wout)]
    for pair in range(pairs):
        moves += [
            (q_hbm.at[:, lanes(pair)], q.at[pair]),
            (k_hbm.at[:, lanes(pair)], kx.at[pair, own]),
            (v_hbm.at[:, lanes(pair)], vx.at[pair, own]),
        ]
    soon = len(moves)
    moves += [(wq_hbm, wq), (wk_hbm, wk), (wv_hbm, wv), (unpatch_hbm, unpatch)]
    loads = [
        pltpu.make_async_copy(src, dst, load_sem.at[n]) for n, (src, dst) in enumerate(moves)
    ]
    for load in loads[:soon]:
        load.start()

    barrier = pltpu.get_barrier_semaphore()
    for mate in (near, far):
        pl.semaphore_signal(barrier, inc=1, device_id=(shard, mate), device_id_type=MESH)

    @pl.when(has_prev)
    def _():
        pl.semaphore_signal(barrier, inc=1, device_id=(shard - 1, me), device_id_type=MESH)

    @pl.when(has_next)
    def _():
        pl.semaphore_signal(barrier, inc=1, device_id=(shard + 1, me), device_id_type=MESH)

    peers = 2 + has_prev.astype(jnp.int32) + has_next.astype(jnp.int32)
    pl.semaphore_wait(barrier, peers)

    def halo(n, src, dst):
        return pltpu.make_async_remote_copy(
            src_ref=src,
            dst_ref=dst,
            send_sem=halo_send.at[n],
            recv_sem=halo_recv.at[n],
            device_id=(shard + 1, me),
            device_id_type=MESH,
        )

    tail = rows - WINDOW
    halos = [halo(0, index_ref, halo_index)]
    for pair in range(pairs):
        for first in (BLOCK, 0):
            for src, dst in ((k_hbm, kx), (v_hbm, vx)):
                halos.append(
                    halo(
                        len(halos),
                        src.at[pl.ds(tail + first, BLOCK), lanes(pair)],
                        dst.at[pair, pl.ds(first, BLOCK)],
                    )
                )

    @pl.when(has_next)
    def _():
        for copy in halos:
            copy.start()

    @pl.when(shard == 0)
    def _():
        kx[:, pl.ds(0, WINDOW), :] = jnp.zeros((pairs, WINDOW, PAIR), BF16)
        vx[:, pl.ds(0, WINDOW), :] = jnp.zeros((pairs, WINDOW, PAIR), BF16)
        halo_index[...] = jnp.zeros_like(halo_index)

    dk[...] = jnp.zeros_like(dk)
    dv[...] = jnp.zeros_like(dv)
    for load in loads[:soon]:
        load.wait()
    for load in loads[soon:]:
        load.start()

    def output_grads(block, carry):
        mine = pl.ds(pl.multiple_of(block * BLOCK, BLOCK), BLOCK)
        heads_grad = dot_nt(dout[mine, :], wout[...]).astype(BF16)
        for pair in range(pairs):
            g[pair, mine, :] = heads_grad[:, pair * PAIR : (pair + 1) * PAIR]
        return carry

    lax.fori_loop(0, rows // BLOCK, output_grads, 0)

    def one_hot(index_row, base):
        slot = lax.broadcasted_iota(jnp.int32, (PATCH_DEV, 128), 0)
        return jnp.where(slot == index_row - base, 1.0, 0.0).astype(BF16)

    first_head = lax.broadcasted_iota(jnp.int32, (CHUNK, PAIR), 1) < HS

    def by_head(rows_of):
        blank = jnp.zeros_like(rows_of)
        return jnp.concatenate(
            [jnp.where(first_head, rows_of, blank), jnp.where(first_head, blank, rows_of)], axis=0
        )

    prev_copies = [
        pltpu.make_async_remote_copy(
            src_ref=prev.at[pair],
            dst_ref=from_next.at[pair],
            send_sem=prev_send.at[pair],
            recv_sem=prev_recv.at[pair],
            device_id=(shard - 1, me),
            device_id_type=MESH,
        )
        for pair in range(pairs)
    ]

    def send_prev(pair):
        base = (shard - 1) * PATCH_DEV
        hot = jnp.concatenate(
            [one_hot(halo_index[pl.ds(4 + c, 1), :], base) for c in range(WINDOW // 128)]
            + [one_hot(index_ref[pl.ds(0, 1), :], base)],
            axis=1,
        )
        span = pl.ds(0, WINDOW + 128)
        prev[pair, :, pl.ds(0, PAIR)] = dot_nn(
            hot[:, WINDOW:], grads[pl.ds(0, 128), lanes(pair)]
        ).astype(BF16)
        terms = jnp.concatenate([dk[pair, span, :], dv[pair, span, :]], axis=1).astype(BF16)
        prev[pair, :, pl.ds(PAIR, 2 * PAIR)] = dot_nn(hot, terms).astype(BF16)
        prev_copies[pair].start()

    top_key = lax.broadcasted_iota(jnp.int32, (CHUNK, 2 * CHUNK), 0)
    query_pos = lax.rem(lax.broadcasted_iota(jnp.int32, (CHUNK, 2 * CHUNK), 1), CHUNK)

    def column(row):
        return jnp.broadcast_to(row, (PAIR, CHUNK)).T

    def one_step(step, carry):
        block = jnp.where(step < 2, 2, jnp.where(step < 6, 1 - lax.rem(step, 2), 3))
        pair = jnp.where((step >= 2) & (step < 6), (step - 2) // 2, lax.rem(step, 2))

        for n in range(4):

            @pl.when((step == 2 + n) & has_prev)
            def _(n=n):
                if n == 0:
                    halos[0].wait_recv()
                halos[1 + 2 * n].wait_recv()
                halos[2 + 2 * n].wait_recv()

        for n in range(pairs):

            @pl.when((step == 4 + 2 * n) & has_prev)
            def _(n=n):
                send_prev(n)

        origin = pl.multiple_of(block * BLOCK, BLOCK)
        window = pl.ds(origin, WINDOW + BLOCK)
        keys_t = kx[pair, window, :].T
        scaled_q, scaled_g = [], []
        for c in range(BLOCK // CHUNK):
            start = pl.multiple_of(origin + c * CHUNK, CHUNK)
            mine = pl.ds(start, CHUNK)
            side_lanes = pl.ds(c * 2 * CHUNK, 2 * CHUNK)
            blocked = jnp.where(shard == 0, jnp.maximum(WINDOW - start, 0), 0)
            q_rows = q[pair, mine, :].astype(F32) * HS**-0.5
            g_rows = g[pair, mine, :]
            queries = by_head(q_rows.astype(BF16))
            grads_in = by_head(g_rows)
            peak = None
            for n in range(PIECES):
                piece = pl.ds(n * CHUNK, CHUNK)
                part = dot_nt(kx[pair, pl.ds(start + n * CHUNK, CHUNK), :], queries)
                if n == 0:
                    part = jnp.where(top_key > jnp.maximum(query_pos, blocked - 1), part, -1e30)
                elif n == PIECES - 1:
                    part = jnp.where(top_key <= query_pos, part, -1e30)
                else:
                    part = jnp.where(top_key >= blocked - n * CHUNK, part, -1e30)
                scores[c, piece, :] = part
                best = jnp.max(part.reshape(CHUNK // 8, 8, 2 * CHUNK), axis=0)
                peak = best if peak is None else jnp.maximum(peak, best)
            peak = jnp.max(peak, axis=0, keepdims=True)
            weight = jnp.zeros((8, 2 * CHUNK), F32)
            mixed = jnp.zeros((8, 2 * CHUNK), F32)
            for n in range(PIECES):
                piece = pl.ds(n * CHUNK, CHUNK)
                raised = jnp.exp(scores[c, piece, :] - peak)
                part = dot_nt(vx[pair, pl.ds(start + n * CHUNK, CHUNK), :], grads_in)
                d_attend[c, piece, :] = part
                p_low[pl.ds((c + n) * CHUNK, CHUNK), side_lanes] = raised.astype(BF16)
                weight += jnp.sum(raised.reshape(CHUNK // 8, 8, 2 * CHUNK), axis=0)
                mixed += jnp.sum((raised * part).reshape(CHUNK // 8, 8, 2 * CHUNK), axis=0)
            inverse = 1.0 / jnp.sum(weight, axis=0, keepdims=True)
            row_dot = jnp.sum(mixed, axis=0, keepdims=True) * inverse
            for n in range(PIECES):
                piece = pl.ds(n * CHUNK, CHUNK)
                place = pl.ds((c + n) * CHUNK, CHUNK)
                ds_low[place, side_lanes] = (
                    p_low[place, side_lanes].astype(F32) * (d_attend[c, piece, :] - row_dot)
                ).astype(BF16)
            scale = jnp.where(
                first_head, column(inverse[:, :CHUNK]), column(inverse[:, CHUNK:])
            )
            scaled_q.append(by_head((q_rows * scale).astype(BF16)))
            scaled_g.append(by_head((g_rows.astype(F32) * scale).astype(BF16)))
            d_query = dot_nn(
                keys_t[:, c * CHUNK : c * CHUNK + SPAN],
                ds_low[pl.ds(c * CHUNK, SPAN), side_lanes],
            ) * (inverse * HS**-0.5)
            d_query = jnp.concatenate([d_query[:HS, :CHUNK], d_query[HS:, CHUNK:]], axis=0)
            grads[mine, pl.ds(pl.multiple_of(pair * PAIR, PAIR), PAIR)] = d_query.T.astype(BF16)
        for held, low, rows_of in ((dk, ds_low, scaled_q), (dv, p_low, scaled_g)):
            held[pair, pl.ds(origin, CHUNK), :] += dot_nn(
                low[pl.ds(0, CHUNK), pl.ds(0, 2 * CHUNK)], rows_of[0]
            )
            held[pair, pl.ds(origin + CHUNK, WINDOW), :] += dot_nn(
                low[pl.ds(CHUNK, WINDOW), :], jnp.concatenate(rows_of, axis=0)
            )
            held[pair, pl.ds(origin + SPAN, CHUNK), :] += dot_nn(
                low[pl.ds(SPAN, CHUNK), pl.ds(2 * CHUNK, 2 * CHUNK)], rows_of[1]
            )
        return carry

    lax.fori_loop(0, rows // BLOCK * pairs, one_step, 0)

    for pair in range(pairs):
        grads[:, pl.ds(width + pair * PAIR, PAIR)] = dk[pair, own, :].astype(BF16)
        grads[:, pl.ds(2 * width + pair * PAIR, PAIR)] = dv[pair, own, :].astype(BF16)
    hot = jnp.concatenate(
        [one_hot(index_ref[pl.ds(c, 1), :], shard * PATCH_DEV) for c in range(rows // 128)],
        axis=1,
    )
    pooled = dot_nn(hot, grads[...])
    for load in loads[soon:]:
        load.wait()

    total[...] = pooled

    @pl.when(has_next)
    def _():
        for pair in range(pairs):
            prev_copies[pair].wait_recv()
            for n in range(3):
                total[:, pl.ds(n * width + pair * PAIR, PAIR)] += from_next[
                    pair, :, pl.ds(n * PAIR, PAIR)
                ].astype(F32)

    def project(first):
        part = total[pl.ds(first, PATCH_DEV // 2), :].astype(BF16)
        return (
            dot_nt(part[:, :width], wq[...])
            + dot_nt(part[:, width : 2 * width], wk[...])
            + dot_nt(part[:, 2 * width :], wv[...])
        )

    side = PATCH_DEV // 2
    part = side // PARTS

    def swap(src, dst, sends, recvs, mate):
        return [
            pltpu.make_async_remote_copy(
                src_ref=src.at[pl.ds(n * part, part)],
                dst_ref=dst.at[pl.ds(n * part, part)],
                send_sem=sends.at[n],
                recv_sem=recvs.at[n],
                device_id=(shard, mate),
                device_id_type=MESH,
            )
            for n in range(PARTS)
        ]

    core_copies = swap(give, take, core_send, core_recv, near)
    far_copies = swap(half, half_in, far_send, far_recv, far)
    near_copies = swap(done, last, near_send, near_recv, near)
    give[...] = project(pl.multiple_of((1 - core) * side, side)).astype(BF16)
    for copy in core_copies:
        copy.start()
    kept[...] = project(pl.multiple_of(core * side, side))
    for n in range(PARTS):
        piece = pl.ds(n * part, part)
        core_copies[n].wait_recv()
        kept[piece, :] += take[piece, :].astype(F32)
        half[piece, :] = kept[piece, :].astype(BF16)
        far_copies[n].start()
    for n in range(PARTS):
        piece = pl.ds(n * part, part)
        far_copies[n].wait_recv()
        done[piece, :] = (kept[piece, :] + half_in[piece, :].astype(F32)).astype(BF16)
        near_copies[n].start()
    out_ref[pl.ds(pl.multiple_of(core * side, side), side), :] = dot_nn(
        done[...], unpatch[...]
    ).astype(BF16)
    for copy in near_copies:
        copy.wait_recv()
    out_ref[pl.ds(pl.multiple_of((1 - core) * side, side), side), :] = dot_nn(
        last[...], unpatch[...]
    ).astype(BF16)
    for copy in core_copies + far_copies + near_copies:
        copy.wait_send()

    @pl.when(has_prev)
    def _():
        for copy in prev_copies:
            copy.wait_send()

    @pl.when(has_next)
    def _():
        for copy in halos:
            copy.wait_send()


def on_device(
    shards,
    queries,
    byte_keys,
    byte_values,
    w_query,
    w_key,
    w_value,
    w_out,
    d_output,
    patch_index,
    unpatch,
):
    rows, width = queries.shape
    full = w_query.shape[0]
    out_width = unpatch.shape[1]
    pairs = width // PAIR
    side = PATCH_DEV // 2
    vmem = pltpu.VMEM
    dma = pltpu.SemaphoreType.DMA
    anywhere = pl.BlockSpec(memory_space=pl.ANY)
    local = pl.BlockSpec(memory_space=pltpu.VMEM)
    return pl.pallas_call(
        functools.partial(kernel, shards),
        out_shape=jax.ShapeDtypeStruct((PATCH_DEV, out_width), BF16),
        in_specs=[anywhere] * 8 + [local, anywhere],
        out_specs=local,
        scratch_shapes=[
            vmem((pairs, rows, PAIR), BF16),
            vmem((pairs, rows + WINDOW, PAIR), BF16),
            vmem((pairs, rows + WINDOW, PAIR), BF16),
            vmem(w_query.shape, BF16),
            vmem(w_key.shape, BF16),
            vmem(w_value.shape, BF16),
            vmem(w_out.shape, BF16),
            vmem(d_output.shape, BF16),
            vmem(unpatch.shape, BF16),
            vmem((pairs, rows, PAIR), BF16),
            vmem((pairs, rows + WINDOW, PAIR), F32),
            vmem((pairs, rows + WINDOW, PAIR), F32),
            vmem((rows, 3 * width), BF16),
            vmem((2, SPAN, 2 * CHUNK), F32),
            vmem((2, SPAN, 2 * CHUNK), F32),
            vmem((SPAN + CHUNK, 4 * CHUNK), BF16),
            vmem((SPAN + CHUNK, 4 * CHUNK), BF16),
            vmem((8, 128), jnp.int32),
            vmem((pairs, PATCH_DEV, 3 * PAIR), BF16),
            vmem((pairs, PATCH_DEV, 3 * PAIR), BF16),
            vmem((side, full), BF16),
            vmem((side, full), BF16),
            vmem((side, full), BF16),
            vmem((side, full), BF16),
            vmem((side, full), BF16),
            vmem((side, full), BF16),
            vmem((side, full), F32),
            vmem((PATCH_DEV, 3 * width), F32),
            dma((6 + 3 * pairs,)),
            dma((1 + 4 * pairs,)),
            dma((1 + 4 * pairs,)),
            dma((pairs,)),
            dma((pairs,)),
            dma((PARTS,)),
            dma((PARTS,)),
            dma((PARTS,)),
            dma((PARTS,)),
            dma((PARTS,)),
            dma((PARTS,)),
        ],
        compiler_params=pltpu.CompilerParams(
            collective_id=0, has_side_effects=True, vmem_limit_bytes=56 * 1024 * 1024
        ),
        name="fused_backward",
    )(
        queries,
        byte_keys,
        byte_values,
        w_query,
        w_key,
        w_value,
        w_out,
        d_output,
        patch_index.reshape(8, 128),
        unpatch,
    )


def solution(mesh):
    in_specs = (
        P("seq", "mp"),
        P("seq", "mp"),
        P("seq", "mp"),
        P(None, "mp"),
        P(None, "mp"),
        P(None, "mp"),
        P("mp", None),
        P("seq", None),
        P("seq"),
        P(None, "mp"),
    )
    return jax.shard_map(
        functools.partial(on_device, mesh.shape["seq"]),
        mesh=mesh,
        in_specs=in_specs,
        out_specs=P("seq", "mp"),
        check_vma=False,
    )
```

```python
import functools

import jax
import jax.numpy as jnp
from jax import lax
from jax.experimental import pallas as pl
from jax.experimental.pallas import tpu as pltpu
from jax.sharding import PartitionSpec as P

HS = 64
WINDOW = 512
PATCH_DEV = 256
BLOCK = 256
CHUNK = 128
SPAN = WINDOW + CHUNK
PAIR = 2 * HS
PARTS = 4
REACH = 128
PIECES = SPAN // CHUNK
MESH = pl.DeviceIdType.MESH
F32 = jnp.float32
BF16 = jnp.bfloat16


def dot_nt(a, b):
    return lax.dot_general(a, b, (((1,), (1,)), ((), ())), preferred_element_type=F32)


def dot_nn(a, b):
    return lax.dot_general(a, b, (((1,), (0,)), ((), ())), preferred_element_type=F32)


def kernel(
    shards,
    q_hbm,
    k_hbm,
    v_hbm,
    wq_hbm,
    wk_hbm,
    wv_hbm,
    wout_hbm,
    dout_hbm,
    index_ref,
    out_ref,
    q,
    kx,
    vx,
    wq,
    wk,
    wv,
    wout,
    dout,
    g,
    dk,
    dv,
    grads,
    scores,
    d_attend,
    p_low,
    ds_low,
    halo_index,
    prev,
    from_next,
    give,
    take,
    half,
    half_in,
    done,
    last,
    kept,
    total,
    load_sem,
    halo_send,
    halo_recv,
    prev_send,
    prev_recv,
    core_send,
    core_recv,
    far_send,
    far_recv,
    near_send,
    near_recv,
):
    rows = q_hbm.shape[0]
    width = q_hbm.shape[1]
    pairs = width // PAIR
    shard = lax.axis_index("seq")
    me = lax.axis_index("mp")
    core = lax.rem(me, 2)
    near = me + 1 - 2 * core
    far = lax.rem(me + 2, 4)
    has_prev = shard > 0
    has_next = shard < shards - 1

    def lanes(pair):
        return pl.ds(pair * PAIR, PAIR)

    own = pl.ds(WINDOW, rows)
    moves = [(dout_hbm, dout), (wout_hbm, wout)]
    for pair in range(pairs):
        moves += [
            (q_hbm.at[:, lanes(pair)], q.at[pair]),
            (k_hbm.at[:, lanes(pair)], kx.at[pair, own]),
            (v_hbm.at[:, lanes(pair)], vx.at[pair, own]),
        ]
    soon = len(moves)
    moves += [(wq_hbm, wq), (wk_hbm, wk), (wv_hbm, wv)]
    loads = [
        pltpu.make_async_copy(src, dst, load_sem.at[n]) for n, (src, dst) in enumerate(moves)
    ]
    for load in loads[:soon]:
        load.start()

    barrier = pltpu.get_barrier_semaphore()
    for mate in (near, far):
        pl.semaphore_signal(barrier, inc=1, device_id=(shard, mate), device_id_type=MESH)

    @pl.when(has_prev)
    def _():
        pl.semaphore_signal(barrier, inc=1, device_id=(shard - 1, me), device_id_type=MESH)

    @pl.when(has_next)
    def _():
        pl.semaphore_signal(barrier, inc=1, device_id=(shard + 1, me), device_id_type=MESH)

    peers = 2 + has_prev.astype(jnp.int32) + has_next.astype(jnp.int32)
    pl.semaphore_wait(barrier, peers)

    def halo(n, src, dst):
        return pltpu.make_async_remote_copy(
            src_ref=src,
            dst_ref=dst,
            send_sem=halo_send.at[n],
            recv_sem=halo_recv.at[n],
            device_id=(shard + 1, me),
            device_id_type=MESH,
        )

    tail = rows - WINDOW
    halos = [halo(0, index_ref, halo_index)]
    for pair in range(pairs):
        for first in (BLOCK, 0):
            for src, dst in ((k_hbm, kx), (v_hbm, vx)):
                halos.append(
                    halo(
                        len(halos),
                        src.at[pl.ds(tail + first, BLOCK), lanes(pair)],
                        dst.at[pair, pl.ds(first, BLOCK)],
                    )
                )

    @pl.when(has_next)
    def _():
        for copy in halos:
            copy.start()

    @pl.when(shard == 0)
    def _():
        kx[:, pl.ds(0, WINDOW), :] = jnp.zeros((pairs, WINDOW, PAIR), BF16)
        vx[:, pl.ds(0, WINDOW), :] = jnp.zeros((pairs, WINDOW, PAIR), BF16)
        halo_index[...] = jnp.zeros_like(halo_index)

    dk[...] = jnp.zeros_like(dk)
    dv[...] = jnp.zeros_like(dv)
    for load in loads[:soon]:
        load.wait()
    for load in loads[soon:]:
        load.start()

    def output_grads(block, carry):
        mine = pl.ds(pl.multiple_of(block * BLOCK, BLOCK), BLOCK)
        heads_grad = dot_nt(dout[mine, :], wout[...]).astype(BF16)
        for pair in range(pairs):
            g[pair, mine, :] = heads_grad[:, pair * PAIR : (pair + 1) * PAIR]
        return carry

    lax.fori_loop(0, rows // BLOCK, output_grads, 0)

    def one_hot(index_row, base):
        slot = lax.broadcasted_iota(jnp.int32, (PATCH_DEV, 128), 0)
        return jnp.where(slot == index_row - base, 1.0, 0.0).astype(BF16)

    first_head = lax.broadcasted_iota(jnp.int32, (CHUNK, PAIR), 1) < HS

    def by_head(rows_of):
        blank = jnp.zeros_like(rows_of)
        return jnp.concatenate(
            [jnp.where(first_head, rows_of, blank), jnp.where(first_head, blank, rows_of)], axis=0
        )

    prev_copies = [
        pltpu.make_async_remote_copy(
            src_ref=prev.at[pair],
            dst_ref=from_next.at[pair],
            send_sem=prev_send.at[pair],
            recv_sem=prev_recv.at[pair],
            device_id=(shard - 1, me),
            device_id_type=MESH,
        )
        for pair in range(pairs)
    ]

    def send_prev(pair):
        base = (shard - 1) * PATCH_DEV
        hot = jnp.concatenate(
            [one_hot(halo_index[pl.ds(4 + c, 1), :], base) for c in range(WINDOW // 128)]
            + [one_hot(index_ref[pl.ds(0, 1), :], base)],
            axis=1,
        )
        span = pl.ds(0, WINDOW + 128)
        terms = jnp.concatenate([dk[pair, span, :], dv[pair, span, :]], axis=1).astype(BF16)
        terms = dot_nn(hot, terms).astype(BF16)
        prev[pair, pl.ds(0, PATCH_DEV), :] = terms[:, :PAIR]
        prev[pair, pl.ds(PATCH_DEV, PATCH_DEV), :] = terms[:, PAIR:]
        prev[pair, pl.ds(2 * PATCH_DEV, REACH), :] = dot_nn(
            hot[PATCH_DEV - REACH :, WINDOW:], grads[pl.ds(0, REACH), lanes(pair)]
        ).astype(BF16)
        prev_copies[pair].start()

    top_key = lax.broadcasted_iota(jnp.int32, (CHUNK, 2 * CHUNK), 0)
    query_pos = lax.rem(lax.broadcasted_iota(jnp.int32, (CHUNK, 2 * CHUNK), 1), CHUNK)

    def column(row):
        return jnp.broadcast_to(row, (PAIR, CHUNK)).T

    def one_step(step, carry):
        block = jnp.where(step < 2, 2, jnp.where(step < 6, 1 - lax.rem(step, 2), 3))
        pair = jnp.where((step >= 2) & (step < 6), (step - 2) // 2, lax.rem(step, 2))

        for n in range(4):

            @pl.when((step == 2 + n) & has_prev)
            def _(n=n):
                if n == 0:
                    halos[0].wait_recv()
                halos[1 + 2 * n].wait_recv()
                halos[2 + 2 * n].wait_recv()

        for n in range(pairs):

            @pl.when((step == 4 + 2 * n) & has_prev)
            def _(n=n):
                send_prev(n)

        origin = pl.multiple_of(block * BLOCK, BLOCK)
        window = pl.ds(origin, WINDOW + BLOCK)
        keys_t = kx[pair, window, :].T
        scaled_q, scaled_g = [], []
        for c in range(BLOCK // CHUNK):
            start = pl.multiple_of(origin + c * CHUNK, CHUNK)
            mine = pl.ds(start, CHUNK)
            side_lanes = pl.ds(c * 2 * CHUNK, 2 * CHUNK)
            blocked = jnp.where(shard == 0, jnp.maximum(WINDOW - start, 0), 0)
            q_rows = q[pair, mine, :].astype(F32) * HS**-0.5
            g_rows = g[pair, mine, :]
            queries = by_head(q_rows.astype(BF16))
            grads_in = by_head(g_rows)
            peak = None
            for n in range(PIECES):
                piece = pl.ds(n * CHUNK, CHUNK)
                part = dot_nt(kx[pair, pl.ds(start + n * CHUNK, CHUNK), :], queries)
                if n == 0:
                    part = jnp.where(top_key > jnp.maximum(query_pos, blocked - 1), part, -1e30)
                elif n == PIECES - 1:
                    part = jnp.where(top_key <= query_pos, part, -1e30)
                else:
                    part = jnp.where(top_key >= blocked - n * CHUNK, part, -1e30)
                scores[c, piece, :] = part
                best = jnp.max(part.reshape(CHUNK // 8, 8, 2 * CHUNK), axis=0)
                peak = best if peak is None else jnp.maximum(peak, best)
            peak = jnp.max(peak, axis=0, keepdims=True)
            weight = jnp.zeros((8, 2 * CHUNK), F32)
            mixed = jnp.zeros((8, 2 * CHUNK), F32)
            for n in range(PIECES):
                piece = pl.ds(n * CHUNK, CHUNK)
                raised = jnp.exp(scores[c, piece, :] - peak)
                part = dot_nt(vx[pair, pl.ds(start + n * CHUNK, CHUNK), :], grads_in)
                d_attend[c, piece, :] = part
                p_low[pl.ds((c + n) * CHUNK, CHUNK), side_lanes] = raised.astype(BF16)
                weight += jnp.sum(raised.reshape(CHUNK // 8, 8, 2 * CHUNK), axis=0)
                mixed += jnp.sum((raised * part).reshape(CHUNK // 8, 8, 2 * CHUNK), axis=0)
            inverse = 1.0 / jnp.sum(weight, axis=0, keepdims=True)
            row_dot = jnp.sum(mixed, axis=0, keepdims=True) * inverse
            for n in range(PIECES):
                piece = pl.ds(n * CHUNK, CHUNK)
                place = pl.ds((c + n) * CHUNK, CHUNK)
                ds_low[place, side_lanes] = (
                    p_low[place, side_lanes].astype(F32) * (d_attend[c, piece, :] - row_dot)
                ).astype(BF16)
            scale = jnp.where(
                first_head, column(inverse[:, :CHUNK]), column(inverse[:, CHUNK:])
            )
            scaled_q.append(by_head((q_rows * scale).astype(BF16)))
            scaled_g.append(by_head((g_rows.astype(F32) * scale).astype(BF16)))
            d_query = dot_nn(
                keys_t[:, c * CHUNK : c * CHUNK + SPAN],
                ds_low[pl.ds(c * CHUNK, SPAN), side_lanes],
            ) * (inverse * HS**-0.5)
            d_query = jnp.concatenate([d_query[:HS, :CHUNK], d_query[HS:, CHUNK:]], axis=0)
            grads[mine, pl.ds(pl.multiple_of(pair * PAIR, PAIR), PAIR)] = d_query.T.astype(BF16)
        for held, low, rows_of in ((dk, ds_low, scaled_q), (dv, p_low, scaled_g)):
            held[pair, pl.ds(origin, CHUNK), :] += dot_nn(
                low[pl.ds(0, CHUNK), pl.ds(0, 2 * CHUNK)], rows_of[0]
            )
            held[pair, pl.ds(origin + CHUNK, WINDOW), :] += dot_nn(
                low[pl.ds(CHUNK, WINDOW), :], jnp.concatenate(rows_of, axis=0)
            )
            held[pair, pl.ds(origin + SPAN, CHUNK), :] += dot_nn(
                low[pl.ds(SPAN, CHUNK), pl.ds(2 * CHUNK, 2 * CHUNK)], rows_of[1]
            )
        return carry

    lax.fori_loop(0, rows // BLOCK * pairs, one_step, 0)

    for pair in range(pairs):
        grads[:, pl.ds(width + pair * PAIR, PAIR)] = dk[pair, own, :].astype(BF16)
        grads[:, pl.ds(2 * width + pair * PAIR, PAIR)] = dv[pair, own, :].astype(BF16)
    hot = jnp.concatenate(
        [one_hot(index_ref[pl.ds(c, 1), :], shard * PATCH_DEV) for c in range(rows // 128)],
        axis=1,
    )
    pooled = dot_nn(hot, grads[...])
    for load in loads[soon:]:
        load.wait()

    total[...] = pooled

    @pl.when(has_next)
    def _():
        for pair in range(pairs):
            prev_copies[pair].wait_recv()
            for n in range(2):
                total[:, pl.ds((n + 1) * width + pair * PAIR, PAIR)] += from_next[
                    pair, pl.ds(n * PATCH_DEV, PATCH_DEV), :
                ].astype(F32)
            total[pl.ds(PATCH_DEV - REACH, REACH), lanes(pair)] += from_next[
                pair, pl.ds(2 * PATCH_DEV, REACH), :
            ].astype(F32)

    def project(first):
        part = total[pl.ds(first, PATCH_DEV // 2), :].astype(BF16)
        return (
            dot_nt(part[:, :width], wq[...])
            + dot_nt(part[:, width : 2 * width], wk[...])
            + dot_nt(part[:, 2 * width :], wv[...])
        )

    side = PATCH_DEV // 2
    part = side // PARTS

    def swap(src, dst, sends, recvs, mate):
        return [
            pltpu.make_async_remote_copy(
                src_ref=src.at[pl.ds(n * part, part)],
                dst_ref=dst.at[pl.ds(n * part, part)],
                send_sem=sends.at[n],
                recv_sem=recvs.at[n],
                device_id=(shard, mate),
                device_id_type=MESH,
            )
            for n in range(PARTS)
        ]

    core_copies = swap(give, take, core_send, core_recv, near)
    far_copies = swap(half, half_in, far_send, far_recv, far)
    near_copies = swap(done, last, near_send, near_recv, near)
    give[...] = project(pl.multiple_of((1 - core) * side, side)).astype(BF16)
    for copy in core_copies:
        copy.start()
    kept[...] = project(pl.multiple_of(core * side, side))
    for n in range(PARTS):
        piece = pl.ds(n * part, part)
        core_copies[n].wait_recv()
        kept[piece, :] += take[piece, :].astype(F32)
        half[piece, :] = kept[piece, :].astype(BF16)
        far_copies[n].start()
    for n in range(PARTS):
        piece = pl.ds(n * part, part)
        far_copies[n].wait_recv()
        done[piece, :] = (kept[piece, :] + half_in[piece, :].astype(F32)).astype(BF16)
        near_copies[n].start()
    out_ref[pl.ds(pl.multiple_of(core * side, side), side), :] = done[...]
    for copy in near_copies:
        copy.wait_recv()
    out_ref[pl.ds(pl.multiple_of((1 - core) * side, side), side), :] = last[...]
    for copy in core_copies + far_copies + near_copies:
        copy.wait_send()

    @pl.when(has_prev)
    def _():
        for copy in prev_copies:
            copy.wait_send()

    @pl.when(has_next)
    def _():
        for copy in halos:
            copy.wait_send()


def last_product(patch_ref, unpatch_ref, out_ref):
    out_ref[...] = dot_nn(patch_ref[...], unpatch_ref[...]).astype(BF16)


def on_device(
    shards,
    queries,
    byte_keys,
    byte_values,
    w_query,
    w_key,
    w_value,
    w_out,
    d_output,
    patch_index,
    unpatch,
):
    rows, width = queries.shape
    full = w_query.shape[0]
    out_width = unpatch.shape[1]
    pairs = width // PAIR
    side = PATCH_DEV // 2
    vmem = pltpu.VMEM
    dma = pltpu.SemaphoreType.DMA
    anywhere = pl.BlockSpec(memory_space=pl.ANY)
    local = pl.BlockSpec(memory_space=pltpu.VMEM)
    patch_grads = pl.pallas_call(
        functools.partial(kernel, shards),
        out_shape=jax.ShapeDtypeStruct((PATCH_DEV, full), BF16),
        in_specs=[anywhere] * 8 + [local],
        out_specs=local,
        scratch_shapes=[
            vmem((pairs, rows, PAIR), BF16),
            vmem((pairs, rows + WINDOW, PAIR), BF16),
            vmem((pairs, rows + WINDOW, PAIR), BF16),
            vmem(w_query.shape, BF16),
            vmem(w_key.shape, BF16),
            vmem(w_value.shape, BF16),
            vmem(w_out.shape, BF16),
            vmem(d_output.shape, BF16),
            vmem((pairs, rows, PAIR), BF16),
            vmem((pairs, rows + WINDOW, PAIR), F32),
            vmem((pairs, rows + WINDOW, PAIR), F32),
            vmem((rows, 3 * width), BF16),
            vmem((2, SPAN, 2 * CHUNK), F32),
            vmem((2, SPAN, 2 * CHUNK), F32),
            vmem((SPAN + CHUNK, 4 * CHUNK), BF16),
            vmem((SPAN + CHUNK, 4 * CHUNK), BF16),
            vmem((8, 128), jnp.int32),
            vmem((pairs, 2 * PATCH_DEV + REACH, PAIR), BF16),
            vmem((pairs, 2 * PATCH_DEV + REACH, PAIR), BF16),
            vmem((side, full), BF16),
            vmem((side, full), BF16),
            vmem((side, full), BF16),
            vmem((side, full), BF16),
            vmem((side, full), BF16),
            vmem((side, full), BF16),
            vmem((side, full), F32),
            vmem((PATCH_DEV, 3 * width), F32),
            dma((5 + 3 * pairs,)),
            dma((1 + 4 * pairs,)),
            dma((1 + 4 * pairs,)),
            dma((pairs,)),
            dma((pairs,)),
            dma((PARTS,)),
            dma((PARTS,)),
            dma((PARTS,)),
            dma((PARTS,)),
            dma((PARTS,)),
            dma((PARTS,)),
        ],
        compiler_params=pltpu.CompilerParams(
            collective_id=0, has_side_effects=True, vmem_limit_bytes=56 * 1024 * 1024
        ),
        name="fused_backward",
    )(
        queries,
        byte_keys,
        byte_values,
        w_query,
        w_key,
        w_value,
        w_out,
        d_output,
        patch_index.reshape(8, 128),
    )
    return pl.pallas_call(
        last_product,
        grid=(out_width // BLOCK,),
        out_shape=jax.ShapeDtypeStruct((PATCH_DEV, out_width), BF16),
        in_specs=[
            pl.BlockSpec((PATCH_DEV, full), lambda n: (0, 0)),
            pl.BlockSpec((full, BLOCK), lambda n: (0, n)),
        ],
        out_specs=pl.BlockSpec((PATCH_DEV, BLOCK), lambda n: (0, n)),
        name="last_product",
    )(patch_grads, unpatch)


def solution(mesh):
    in_specs = (
        P("seq", "mp"),
        P("seq", "mp"),
        P("seq", "mp"),
        P(None, "mp"),
        P(None, "mp"),
        P(None, "mp"),
        P("mp", None),
        P("seq", None),
        P("seq"),
        P(None, "mp"),
    )
    return jax.shard_map(
        functools.partial(on_device, mesh.shape["seq"]),
        mesh=mesh,
        in_specs=in_specs,
        out_specs=P("seq", "mp"),
        check_vma=False,
    )
```

```python
import functools

import jax
import jax.numpy as jnp
from jax import lax
from jax.experimental import pallas as pl
from jax.experimental.pallas import tpu as pltpu
from jax.sharding import PartitionSpec as P

HS = 64
WINDOW = 512
PATCH_DEV = 256
BLOCK = 256
CHUNK = 128
SPAN = WINDOW + CHUNK
PAIR = 2 * HS
PARTS = 4
REACH = 128
PIECES = SPAN // CHUNK
MESH = pl.DeviceIdType.MESH
F32 = jnp.float32
BF16 = jnp.bfloat16


def dot_nt(a, b):
    return lax.dot_general(a, b, (((1,), (1,)), ((), ())), preferred_element_type=F32)


def dot_nn(a, b):
    return lax.dot_general(a, b, (((1,), (0,)), ((), ())), preferred_element_type=F32)


def kernel(
    shards,
    q_hbm,
    k_hbm,
    v_hbm,
    wq_hbm,
    wk_hbm,
    wv_hbm,
    wout_hbm,
    dout_hbm,
    index_ref,
    unpatch_hbm,
    out_ref,
    q,
    kx,
    vx,
    wq,
    wk,
    wv,
    wout,
    dout,
    unpatch,
    g,
    dk,
    dv,
    grads,
    scores,
    d_attend,
    p_low,
    ds_low,
    halo_index,
    prev,
    from_next,
    give,
    take,
    half,
    half_in,
    done,
    last,
    kept,
    total,
    load_sem,
    halo_send,
    halo_recv,
    prev_send,
    prev_recv,
    core_send,
    core_recv,
    far_send,
    far_recv,
    near_send,
    near_recv,
):
    rows = q_hbm.shape[0]
    width = q_hbm.shape[1]
    pairs = width // PAIR
    shard = lax.axis_index("seq")
    me = lax.axis_index("mp")
    core = lax.rem(me, 2)
    near = me + 1 - 2 * core
    far = lax.rem(me + 2, 4)
    has_prev = shard > 0
    has_next = shard < shards - 1

    def lanes(pair):
        return pl.ds(pair * PAIR, PAIR)

    own = pl.ds(WINDOW, rows)
    tail = rows - WINDOW
    moves = []
    for pair in range(pairs):
        for src, dst in ((k_hbm, kx), (v_hbm, vx)):
            moves.append((src.at[pl.ds(tail, WINDOW), lanes(pair)], dst.at[pair, pl.ds(rows, WINDOW)]))
    first_moves = len(moves)
    for pair in range(pairs):
        for src, dst in ((k_hbm, kx), (v_hbm, vx)):
            moves.append((src.at[pl.ds(0, tail), lanes(pair)], dst.at[pair, pl.ds(WINDOW, tail)]))
    moves.append((wout_hbm, wout))
    for pair in range(pairs):
        moves.append((q_hbm.at[:, lanes(pair)], q.at[pair]))
    output_moves = len(moves)
    for n in range(rows // BLOCK):
        mine = pl.ds(n * BLOCK, BLOCK)
        moves.append((dout_hbm.at[mine], dout.at[mine]))
    soon = len(moves)
    moves += [(wq_hbm, wq), (wk_hbm, wk), (wv_hbm, wv), (unpatch_hbm, unpatch)]
    loads = [
        pltpu.make_async_copy(src, dst, load_sem.at[n]) for n, (src, dst) in enumerate(moves)
    ]
    for load in loads[:soon]:
        load.start()

    barrier = pltpu.get_barrier_semaphore()
    for mate in (near, far):
        pl.semaphore_signal(barrier, inc=1, device_id=(shard, mate), device_id_type=MESH)

    @pl.when(has_prev)
    def _():
        pl.semaphore_signal(barrier, inc=1, device_id=(shard - 1, me), device_id_type=MESH)

    @pl.when(has_next)
    def _():
        pl.semaphore_signal(barrier, inc=1, device_id=(shard + 1, me), device_id_type=MESH)

    peers = 2 + has_prev.astype(jnp.int32) + has_next.astype(jnp.int32)
    pl.semaphore_wait(barrier, peers)

    def halo(n, src, dst):
        return pltpu.make_async_remote_copy(
            src_ref=src,
            dst_ref=dst,
            send_sem=halo_send.at[n],
            recv_sem=halo_recv.at[n],
            device_id=(shard + 1, me),
            device_id_type=MESH,
        )

    halos = [halo(0, index_ref, halo_index)]
    for pair in range(pairs):
        for first in (BLOCK, 0):
            for held in (kx, vx):
                halos.append(
                    halo(
                        len(halos),
                        held.at[pair, pl.ds(rows + first, BLOCK)],
                        held.at[pair, pl.ds(first, BLOCK)],
                    )
                )
    for load in loads[:first_moves]:
        load.wait()

    @pl.when(has_next)
    def _():
        for copy in halos:
            copy.start()

    @pl.when(shard == 0)
    def _():
        kx[:, pl.ds(0, WINDOW), :] = jnp.zeros((pairs, WINDOW, PAIR), BF16)
        vx[:, pl.ds(0, WINDOW), :] = jnp.zeros((pairs, WINDOW, PAIR), BF16)
        halo_index[...] = jnp.zeros_like(halo_index)

    dk[...] = jnp.zeros_like(dk)
    dv[...] = jnp.zeros_like(dv)
    for load in loads[first_moves:output_moves]:
        load.wait()

    for n in range(rows // BLOCK):
        loads[output_moves + n].wait()
        mine = pl.ds(n * BLOCK, BLOCK)
        heads_grad = dot_nt(dout[mine, :], wout[...]).astype(BF16)
        for pair in range(pairs):
            g[pair, mine, :] = heads_grad[:, pair * PAIR : (pair + 1) * PAIR]
    for load in loads[soon:]:
        load.start()

    def one_hot(index_row, base):
        slot = lax.broadcasted_iota(jnp.int32, (PATCH_DEV, 128), 0)
        return jnp.where(slot == index_row - base, 1.0, 0.0).astype(BF16)

    first_head = lax.broadcasted_iota(jnp.int32, (CHUNK, PAIR), 1) < HS

    def by_head(rows_of):
        blank = jnp.zeros_like(rows_of)
        return jnp.concatenate(
            [jnp.where(first_head, rows_of, blank), jnp.where(first_head, blank, rows_of)], axis=0
        )

    prev_copies = [
        pltpu.make_async_remote_copy(
            src_ref=prev.at[pair],
            dst_ref=from_next.at[pair],
            send_sem=prev_send.at[pair],
            recv_sem=prev_recv.at[pair],
            device_id=(shard - 1, me),
            device_id_type=MESH,
        )
        for pair in range(pairs)
    ]

    def send_prev(pair):
        base = (shard - 1) * PATCH_DEV
        hot = jnp.concatenate(
            [one_hot(halo_index[pl.ds(4 + c, 1), :], base) for c in range(WINDOW // 128)]
            + [one_hot(index_ref[pl.ds(0, 1), :], base)],
            axis=1,
        )
        span = pl.ds(0, WINDOW + 128)
        terms = jnp.concatenate([dk[pair, span, :], dv[pair, span, :]], axis=1).astype(BF16)
        terms = dot_nn(hot, terms).astype(BF16)
        prev[pair, pl.ds(0, PATCH_DEV), :] = terms[:, :PAIR]
        prev[pair, pl.ds(PATCH_DEV, PATCH_DEV), :] = terms[:, PAIR:]
        prev[pair, pl.ds(2 * PATCH_DEV, REACH), :] = dot_nn(
            hot[PATCH_DEV - REACH :, WINDOW:], grads[pl.ds(0, REACH), lanes(pair)]
        ).astype(BF16)
        prev_copies[pair].start()

    top_key = lax.broadcasted_iota(jnp.int32, (CHUNK, 2 * CHUNK), 0)
    query_pos = lax.rem(lax.broadcasted_iota(jnp.int32, (CHUNK, 2 * CHUNK), 1), CHUNK)

    def column(row):
        return jnp.broadcast_to(row, (PAIR, CHUNK)).T

    def one_step(step, carry):
        block = jnp.where(step < 2, 2, jnp.where(step < 6, 1 - lax.rem(step, 2), 3))
        pair = jnp.where((step >= 2) & (step < 6), (step - 2) // 2, lax.rem(step, 2))

        for n in range(4):

            @pl.when((step == 2 + n) & has_prev)
            def _(n=n):
                if n == 0:
                    halos[0].wait_recv()
                halos[1 + 2 * n].wait_recv()
                halos[2 + 2 * n].wait_recv()

        for n in range(pairs):

            @pl.when((step == 4 + 2 * n) & has_prev)
            def _(n=n):
                send_prev(n)

        origin = pl.multiple_of(block * BLOCK, BLOCK)
        window = pl.ds(origin, WINDOW + BLOCK)
        keys_t = kx[pair, window, :].T
        scaled_q, scaled_g = [], []
        for c in range(BLOCK // CHUNK):
            start = pl.multiple_of(origin + c * CHUNK, CHUNK)
            mine = pl.ds(start, CHUNK)
            side_lanes = pl.ds(c * 2 * CHUNK, 2 * CHUNK)
            blocked = jnp.where(shard == 0, jnp.maximum(WINDOW - start, 0), 0)
            q_rows = q[pair, mine, :].astype(F32) * HS**-0.5
            g_rows = g[pair, mine, :]
            queries = by_head(q_rows.astype(BF16))
            grads_in = by_head(g_rows)
            peak = None
            for n in range(PIECES):
                piece = pl.ds(n * CHUNK, CHUNK)
                part = dot_nt(kx[pair, pl.ds(start + n * CHUNK, CHUNK), :], queries)
                if n == 0:
                    part = jnp.where(top_key > jnp.maximum(query_pos, blocked - 1), part, -1e30)
                elif n == PIECES - 1:
                    part = jnp.where(top_key <= query_pos, part, -1e30)
                else:
                    part = jnp.where(top_key >= blocked - n * CHUNK, part, -1e30)
                scores[c, piece, :] = part
                best = jnp.max(part.reshape(CHUNK // 8, 8, 2 * CHUNK), axis=0)
                peak = best if peak is None else jnp.maximum(peak, best)
            peak = jnp.max(peak, axis=0, keepdims=True)
            weight = jnp.zeros((8, 2 * CHUNK), F32)
            mixed = jnp.zeros((8, 2 * CHUNK), F32)
            for n in range(PIECES):
                piece = pl.ds(n * CHUNK, CHUNK)
                raised = jnp.exp(scores[c, piece, :] - peak)
                part = dot_nt(vx[pair, pl.ds(start + n * CHUNK, CHUNK), :], grads_in)
                d_attend[c, piece, :] = part
                p_low[pl.ds((c + n) * CHUNK, CHUNK), side_lanes] = raised.astype(BF16)
                weight += jnp.sum(raised.reshape(CHUNK // 8, 8, 2 * CHUNK), axis=0)
                mixed += jnp.sum((raised * part).reshape(CHUNK // 8, 8, 2 * CHUNK), axis=0)
            inverse = 1.0 / jnp.sum(weight, axis=0, keepdims=True)
            row_dot = jnp.sum(mixed, axis=0, keepdims=True) * inverse
            for n in range(PIECES):
                piece = pl.ds(n * CHUNK, CHUNK)
                place = pl.ds((c + n) * CHUNK, CHUNK)
                ds_low[place, side_lanes] = (
                    p_low[place, side_lanes].astype(F32) * (d_attend[c, piece, :] - row_dot)
                ).astype(BF16)
            scale = jnp.where(
                first_head, column(inverse[:, :CHUNK]), column(inverse[:, CHUNK:])
            )
            scaled_q.append(by_head((q_rows * scale).astype(BF16)))
            scaled_g.append(by_head((g_rows.astype(F32) * scale).astype(BF16)))
            d_query = dot_nn(
                keys_t[:, c * CHUNK : c * CHUNK + SPAN],
                ds_low[pl.ds(c * CHUNK, SPAN), side_lanes],
            ) * (inverse * HS**-0.5)
            d_query = jnp.concatenate([d_query[:HS, :CHUNK], d_query[HS:, CHUNK:]], axis=0)
            grads[mine, pl.ds(pl.multiple_of(pair * PAIR, PAIR), PAIR)] = d_query.T.astype(BF16)
        for held, low, rows_of in ((dk, ds_low, scaled_q), (dv, p_low, scaled_g)):
            held[pair, pl.ds(origin, CHUNK), :] += dot_nn(
                low[pl.ds(0, CHUNK), pl.ds(0, 2 * CHUNK)], rows_of[0]
            )
            held[pair, pl.ds(origin + CHUNK, WINDOW), :] += dot_nn(
                low[pl.ds(CHUNK, WINDOW), :], jnp.concatenate(rows_of, axis=0)
            )
            held[pair, pl.ds(origin + SPAN, CHUNK), :] += dot_nn(
                low[pl.ds(SPAN, CHUNK), pl.ds(2 * CHUNK, 2 * CHUNK)], rows_of[1]
            )
        return carry

    lax.fori_loop(0, rows // BLOCK * pairs, one_step, 0)

    for pair in range(pairs):
        grads[:, pl.ds(width + pair * PAIR, PAIR)] = dk[pair, own, :].astype(BF16)
        grads[:, pl.ds(2 * width + pair * PAIR, PAIR)] = dv[pair, own, :].astype(BF16)
    hot = jnp.concatenate(
        [one_hot(index_ref[pl.ds(c, 1), :], shard * PATCH_DEV) for c in range(rows // 128)],
        axis=1,
    )
    pooled = dot_nn(hot, grads[...])
    for load in loads[soon:]:
        load.wait()

    total[...] = pooled

    @pl.when(has_next)
    def _():
        for pair in range(pairs):
            prev_copies[pair].wait_recv()
            for n in range(2):
                total[:, pl.ds((n + 1) * width + pair * PAIR, PAIR)] += from_next[
                    pair, pl.ds(n * PATCH_DEV, PATCH_DEV), :
                ].astype(F32)
            total[pl.ds(PATCH_DEV - REACH, REACH), lanes(pair)] += from_next[
                pair, pl.ds(2 * PATCH_DEV, REACH), :
            ].astype(F32)

    def project(first):
        part = total[pl.ds(first, PATCH_DEV // 2), :].astype(BF16)
        return (
            dot_nt(part[:, :width], wq[...])
            + dot_nt(part[:, width : 2 * width], wk[...])
            + dot_nt(part[:, 2 * width :], wv[...])
        )

    side = PATCH_DEV // 2
    part = side // PARTS

    def swap(src, dst, sends, recvs, mate):
        return [
            pltpu.make_async_remote_copy(
                src_ref=src.at[pl.ds(n * part, part)],
                dst_ref=dst.at[pl.ds(n * part, part)],
                send_sem=sends.at[n],
                recv_sem=recvs.at[n],
                device_id=(shard, mate),
                device_id_type=MESH,
            )
            for n in range(PARTS)
        ]

    core_copies = swap(give, take, core_send, core_recv, near)
    far_copies = swap(half, half_in, far_send, far_recv, far)
    near_copies = swap(done, last, near_send, near_recv, near)
    give[...] = project(pl.multiple_of((1 - core) * side, side)).astype(BF16)
    for copy in core_copies:
        copy.start()
    kept[...] = project(pl.multiple_of(core * side, side))
    for n in range(PARTS):
        piece = pl.ds(n * part, part)
        core_copies[n].wait_recv()
        kept[piece, :] += take[piece, :].astype(F32)
        half[piece, :] = kept[piece, :].astype(BF16)
        far_copies[n].start()
    for n in range(PARTS):
        piece = pl.ds(n * part, part)
        far_copies[n].wait_recv()
        done[piece, :] = (kept[piece, :] + half_in[piece, :].astype(F32)).astype(BF16)
        near_copies[n].start()
    out_ref[pl.ds(pl.multiple_of(core * side, side), side), :] = dot_nn(
        done[...], unpatch[...]
    ).astype(BF16)
    for copy in near_copies:
        copy.wait_recv()
    out_ref[pl.ds(pl.multiple_of((1 - core) * side, side), side), :] = dot_nn(
        last[...], unpatch[...]
    ).astype(BF16)
    for copy in core_copies + far_copies + near_copies:
        copy.wait_send()

    @pl.when(has_prev)
    def _():
        for copy in prev_copies:
            copy.wait_send()

    @pl.when(has_next)
    def _():
        for copy in halos:
            copy.wait_send()


def on_device(
    shards,
    queries,
    byte_keys,
    byte_values,
    w_query,
    w_key,
    w_value,
    w_out,
    d_output,
    patch_index,
    unpatch,
):
    rows, width = queries.shape
    full = w_query.shape[0]
    out_width = unpatch.shape[1]
    pairs = width // PAIR
    side = PATCH_DEV // 2
    vmem = pltpu.VMEM
    dma = pltpu.SemaphoreType.DMA
    anywhere = pl.BlockSpec(memory_space=pl.ANY)
    local = pl.BlockSpec(memory_space=pltpu.VMEM)
    return pl.pallas_call(
        functools.partial(kernel, shards),
        out_shape=jax.ShapeDtypeStruct((PATCH_DEV, out_width), BF16),
        in_specs=[anywhere] * 8 + [local, anywhere],
        out_specs=local,
        scratch_shapes=[
            vmem((pairs, rows, PAIR), BF16),
            vmem((pairs, rows + WINDOW, PAIR), BF16),
            vmem((pairs, rows + WINDOW, PAIR), BF16),
            vmem(w_query.shape, BF16),
            vmem(w_key.shape, BF16),
            vmem(w_value.shape, BF16),
            vmem(w_out.shape, BF16),
            vmem(d_output.shape, BF16),
            vmem(unpatch.shape, BF16),
            vmem((pairs, rows, PAIR), BF16),
            vmem((pairs, rows + WINDOW, PAIR), F32),
            vmem((pairs, rows + WINDOW, PAIR), F32),
            vmem((rows, 3 * width), BF16),
            vmem((2, SPAN, 2 * CHUNK), F32),
            vmem((2, SPAN, 2 * CHUNK), F32),
            vmem((SPAN + CHUNK, 4 * CHUNK), BF16),
            vmem((SPAN + CHUNK, 4 * CHUNK), BF16),
            vmem((8, 128), jnp.int32),
            vmem((pairs, 2 * PATCH_DEV + REACH, PAIR), BF16),
            vmem((pairs, 2 * PATCH_DEV + REACH, PAIR), BF16),
            vmem((side, full), BF16),
            vmem((side, full), BF16),
            vmem((side, full), BF16),
            vmem((side, full), BF16),
            vmem((side, full), BF16),
            vmem((side, full), BF16),
            vmem((side, full), F32),
            vmem((PATCH_DEV, 3 * width), F32),
            dma((5 + 5 * pairs + rows // BLOCK,)),
            dma((1 + 4 * pairs,)),
            dma((1 + 4 * pairs,)),
            dma((pairs,)),
            dma((pairs,)),
            dma((PARTS,)),
            dma((PARTS,)),
            dma((PARTS,)),
            dma((PARTS,)),
            dma((PARTS,)),
            dma((PARTS,)),
        ],
        compiler_params=pltpu.CompilerParams(
            collective_id=0, has_side_effects=True, vmem_limit_bytes=56 * 1024 * 1024
        ),
        name="fused_backward",
    )(
        queries,
        byte_keys,
        byte_values,
        w_query,
        w_key,
        w_value,
        w_out,
        d_output,
        patch_index.reshape(8, 128),
        unpatch,
    )


def solution(mesh):
    in_specs = (
        P("seq", "mp"),
        P("seq", "mp"),
        P("seq", "mp"),
        P(None, "mp"),
        P(None, "mp"),
        P(None, "mp"),
        P("mp", None),
        P("seq", None),
        P("seq"),
        P(None, "mp"),
    )
    return jax.shard_map(
        functools.partial(on_device, mesh.shape["seq"]),
        mesh=mesh,
        in_specs=in_specs,
        out_specs=P("seq", "mp"),
        check_vma=False,
    )
```

```python
import functools

import jax
import jax.numpy as jnp
from jax import lax
from jax.experimental import pallas as pl
from jax.experimental.pallas import tpu as pltpu
from jax.sharding import PartitionSpec as P

HS = 64
WINDOW = 512
PATCH_DEV = 256
BLOCK = 256
CHUNK = 128
SPAN = WINDOW + CHUNK
PAIR = 2 * HS
PARTS = 4
REACH = 128
PIECES = SPAN // CHUNK
MESH = pl.DeviceIdType.MESH
F32 = jnp.float32
BF16 = jnp.bfloat16


def dot_nt(a, b):
    return lax.dot_general(a, b, (((1,), (1,)), ((), ())), preferred_element_type=F32)


def dot_nn(a, b):
    return lax.dot_general(a, b, (((1,), (0,)), ((), ())), preferred_element_type=F32)


def kernel(
    shards,
    q_hbm,
    k_hbm,
    v_hbm,
    wq_hbm,
    wk_hbm,
    wv_hbm,
    wout_hbm,
    dout_hbm,
    index_ref,
    unpatch_hbm,
    out_ref,
    q,
    kx,
    vx,
    weights,
    wout,
    dout,
    unpatch,
    g,
    dk,
    dv,
    grads,
    scores,
    d_attend,
    p_low,
    ds_low,
    halo_index,
    prev,
    from_next,
    give,
    take,
    half,
    half_in,
    done,
    last,
    kept,
    total,
    load_sem,
    halo_send,
    halo_recv,
    prev_send,
    prev_recv,
    core_send,
    core_recv,
    far_send,
    far_recv,
    near_send,
    near_recv,
):
    rows = q_hbm.shape[0]
    width = q_hbm.shape[1]
    pairs = width // PAIR
    shard = lax.axis_index("seq")
    me = lax.axis_index("mp")
    core = lax.rem(me, 2)
    near = me + 1 - 2 * core
    far = lax.rem(me + 2, 4)
    has_prev = shard > 0
    has_next = shard < shards - 1

    def lanes(pair):
        return pl.ds(pair * PAIR, PAIR)

    own = pl.ds(WINDOW, rows)
    tail = rows - WINDOW
    moves = []
    for pair in range(pairs):
        for src, dst in ((k_hbm, kx), (v_hbm, vx)):
            moves.append((src.at[pl.ds(tail, WINDOW), lanes(pair)], dst.at[pair, pl.ds(rows, WINDOW)]))
    first_moves = len(moves)
    for pair in range(pairs):
        for src, dst in ((k_hbm, kx), (v_hbm, vx)):
            moves.append((src.at[pl.ds(0, tail), lanes(pair)], dst.at[pair, pl.ds(WINDOW, tail)]))
    moves.append((wout_hbm, wout))
    for pair in range(pairs):
        moves.append((q_hbm.at[:, lanes(pair)], q.at[pair]))
    output_moves = len(moves)
    for n in range(rows // BLOCK):
        mine = pl.ds(n * BLOCK, BLOCK)
        moves.append((dout_hbm.at[mine], dout.at[mine]))
    soon = len(moves)
    moves += [
        (src, weights.at[:, pl.ds(n * width, width)])
        for n, src in enumerate((wq_hbm, wk_hbm, wv_hbm))
    ]
    moves.append((unpatch_hbm, unpatch))
    loads = [
        pltpu.make_async_copy(src, dst, load_sem.at[n]) for n, (src, dst) in enumerate(moves)
    ]
    for load in loads[:soon]:
        load.start()

    barrier = pltpu.get_barrier_semaphore()
    for mate in (near, far):
        pl.semaphore_signal(barrier, inc=1, device_id=(shard, mate), device_id_type=MESH)

    @pl.when(has_prev)
    def _():
        pl.semaphore_signal(barrier, inc=1, device_id=(shard - 1, me), device_id_type=MESH)

    @pl.when(has_next)
    def _():
        pl.semaphore_signal(barrier, inc=1, device_id=(shard + 1, me), device_id_type=MESH)

    peers = 2 + has_prev.astype(jnp.int32) + has_next.astype(jnp.int32)
    pl.semaphore_wait(barrier, peers)

    def halo(n, src, dst):
        return pltpu.make_async_remote_copy(
            src_ref=src,
            dst_ref=dst,
            send_sem=halo_send.at[n],
            recv_sem=halo_recv.at[n],
            device_id=(shard + 1, me),
            device_id_type=MESH,
        )

    halos = [halo(0, index_ref, halo_index)]
    for pair in range(pairs):
        for first in (BLOCK, 0):
            for held in (kx, vx):
                halos.append(
                    halo(
                        len(halos),
                        held.at[pair, pl.ds(rows + first, BLOCK)],
                        held.at[pair, pl.ds(first, BLOCK)],
                    )
                )
    for load in loads[:first_moves]:
        load.wait()

    @pl.when(has_next)
    def _():
        for copy in halos:
            copy.start()

    @pl.when(shard == 0)
    def _():
        kx[:, pl.ds(0, WINDOW), :] = jnp.zeros((pairs, WINDOW, PAIR), BF16)
        vx[:, pl.ds(0, WINDOW), :] = jnp.zeros((pairs, WINDOW, PAIR), BF16)
        halo_index[...] = jnp.zeros_like(halo_index)

    dk[...] = jnp.zeros_like(dk)
    dv[...] = jnp.zeros_like(dv)
    for load in loads[first_moves:output_moves]:
        load.wait()

    for n in range(rows // BLOCK):
        loads[output_moves + n].wait()
        mine = pl.ds(n * BLOCK, BLOCK)
        heads_grad = dot_nt(dout[mine, :], wout[...]).astype(BF16)
        for pair in range(pairs):
            g[pair, mine, :] = heads_grad[:, pair * PAIR : (pair + 1) * PAIR]
    for load in loads[soon:]:
        load.start()

    def one_hot(index_row, base):
        slot = lax.broadcasted_iota(jnp.int32, (PATCH_DEV, 128), 0)
        return jnp.where(slot == index_row - base, 1.0, 0.0).astype(BF16)

    first_head = lax.broadcasted_iota(jnp.int32, (CHUNK, PAIR), 1) < HS

    def by_head(rows_of):
        blank = jnp.zeros_like(rows_of)
        return jnp.concatenate(
            [jnp.where(first_head, rows_of, blank), jnp.where(first_head, blank, rows_of)], axis=0
        )

    prev_copies = [
        pltpu.make_async_remote_copy(
            src_ref=prev.at[pair],
            dst_ref=from_next.at[pair],
            send_sem=prev_send.at[pair],
            recv_sem=prev_recv.at[pair],
            device_id=(shard - 1, me),
            device_id_type=MESH,
        )
        for pair in range(pairs)
    ]

    def send_prev(pair):
        base = (shard - 1) * PATCH_DEV
        hot = jnp.concatenate(
            [one_hot(halo_index[pl.ds(4 + c, 1), :], base) for c in range(WINDOW // 128)]
            + [one_hot(index_ref[pl.ds(0, 1), :], base)],
            axis=1,
        )
        span = pl.ds(0, WINDOW + 128)
        terms = jnp.concatenate([dk[pair, span, :], dv[pair, span, :]], axis=1).astype(BF16)
        terms = dot_nn(hot, terms).astype(BF16)
        prev[pair, pl.ds(0, PATCH_DEV), :] = terms[:, :PAIR]
        prev[pair, pl.ds(PATCH_DEV, PATCH_DEV), :] = terms[:, PAIR:]
        prev[pair, pl.ds(2 * PATCH_DEV, REACH), :] = dot_nn(
            hot[PATCH_DEV - REACH :, WINDOW:], grads[pl.ds(0, REACH), lanes(pair)]
        ).astype(BF16)
        prev_copies[pair].start()

    top_key = lax.broadcasted_iota(jnp.int32, (CHUNK, 2 * CHUNK), 0)
    query_pos = lax.rem(lax.broadcasted_iota(jnp.int32, (CHUNK, 2 * CHUNK), 1), CHUNK)

    def column(row):
        return jnp.broadcast_to(row, (PAIR, CHUNK)).T

    def one_step(step, carry):
        block = jnp.where(step < 2, 2, jnp.where(step < 6, 1 - lax.rem(step, 2), 3))
        pair = jnp.where((step >= 2) & (step < 6), (step - 2) // 2, lax.rem(step, 2))

        for n in range(4):

            @pl.when((step == 2 + n) & has_prev)
            def _(n=n):
                if n == 0:
                    halos[0].wait_recv()
                halos[1 + 2 * n].wait_recv()
                halos[2 + 2 * n].wait_recv()

        for n in range(pairs):

            @pl.when((step == 4 + 2 * n) & has_prev)
            def _(n=n):
                send_prev(n)

        origin = pl.multiple_of(block * BLOCK, BLOCK)
        window = pl.ds(origin, WINDOW + BLOCK)
        keys_t = kx[pair, window, :].T
        scaled_q, scaled_g = [], []
        for c in range(BLOCK // CHUNK):
            start = pl.multiple_of(origin + c * CHUNK, CHUNK)
            mine = pl.ds(start, CHUNK)
            side_lanes = pl.ds(c * 2 * CHUNK, 2 * CHUNK)
            blocked = jnp.where(shard == 0, jnp.maximum(WINDOW - start, 0), 0)
            q_rows = q[pair, mine, :].astype(F32) * HS**-0.5
            g_rows = g[pair, mine, :]
            queries = by_head(q_rows.astype(BF16))
            grads_in = by_head(g_rows)
            raw = dot_nt(kx[pair, pl.ds(start, SPAN), :], queries)
            peak = None
            for n in range(PIECES):
                piece = pl.ds(n * CHUNK, CHUNK)
                part = raw[n * CHUNK : (n + 1) * CHUNK, :]
                if n == 0:
                    part = jnp.where(top_key > jnp.maximum(query_pos, blocked - 1), part, -1e30)
                elif n == PIECES - 1:
                    part = jnp.where(top_key <= query_pos, part, -1e30)
                else:
                    part = jnp.where(top_key >= blocked - n * CHUNK, part, -1e30)
                scores[c, piece, :] = part
                best = jnp.max(part.reshape(CHUNK // 8, 8, 2 * CHUNK), axis=0)
                peak = best if peak is None else jnp.maximum(peak, best)
            peak = jnp.max(peak, axis=0, keepdims=True)
            weight = jnp.zeros((8, 2 * CHUNK), F32)
            mixed = jnp.zeros((8, 2 * CHUNK), F32)
            raw = dot_nt(vx[pair, pl.ds(start, SPAN), :], grads_in)
            for n in range(PIECES):
                piece = pl.ds(n * CHUNK, CHUNK)
                raised = jnp.exp(scores[c, piece, :] - peak)
                part = raw[n * CHUNK : (n + 1) * CHUNK, :]
                d_attend[c, piece, :] = part
                p_low[pl.ds((c + n) * CHUNK, CHUNK), side_lanes] = raised.astype(BF16)
                weight += jnp.sum(raised.reshape(CHUNK // 8, 8, 2 * CHUNK), axis=0)
                mixed += jnp.sum((raised * part).reshape(CHUNK // 8, 8, 2 * CHUNK), axis=0)
            inverse = 1.0 / jnp.sum(weight, axis=0, keepdims=True)
            row_dot = jnp.sum(mixed, axis=0, keepdims=True) * inverse
            for n in range(PIECES):
                piece = pl.ds(n * CHUNK, CHUNK)
                place = pl.ds((c + n) * CHUNK, CHUNK)
                ds_low[place, side_lanes] = (
                    p_low[place, side_lanes].astype(F32) * (d_attend[c, piece, :] - row_dot)
                ).astype(BF16)
            scale = jnp.where(
                first_head, column(inverse[:, :CHUNK]), column(inverse[:, CHUNK:])
            )
            scaled_q.append(by_head((q_rows * scale).astype(BF16)))
            scaled_g.append(by_head((g_rows.astype(F32) * scale).astype(BF16)))
            d_query = dot_nn(
                keys_t[:, c * CHUNK : c * CHUNK + SPAN],
                ds_low[pl.ds(c * CHUNK, SPAN), side_lanes],
            ) * (inverse * HS**-0.5)
            d_query = jnp.concatenate([d_query[:HS, :CHUNK], d_query[HS:, CHUNK:]], axis=0)
            grads[mine, pl.ds(pl.multiple_of(pair * PAIR, PAIR), PAIR)] = d_query.T.astype(BF16)
        for held, low, rows_of in ((dk, ds_low, scaled_q), (dv, p_low, scaled_g)):
            held[pair, pl.ds(origin, CHUNK), :] += dot_nn(
                low[pl.ds(0, CHUNK), pl.ds(0, 2 * CHUNK)], rows_of[0]
            )
            held[pair, pl.ds(origin + CHUNK, WINDOW), :] += dot_nn(
                low[pl.ds(CHUNK, WINDOW), :], jnp.concatenate(rows_of, axis=0)
            )
            held[pair, pl.ds(origin + SPAN, CHUNK), :] += dot_nn(
                low[pl.ds(SPAN, CHUNK), pl.ds(2 * CHUNK, 2 * CHUNK)], rows_of[1]
            )
        return carry

    lax.fori_loop(0, rows // BLOCK * pairs, one_step, 0)

    for pair in range(pairs):
        grads[:, pl.ds(width + pair * PAIR, PAIR)] = dk[pair, own, :].astype(BF16)
        grads[:, pl.ds(2 * width + pair * PAIR, PAIR)] = dv[pair, own, :].astype(BF16)
    hot = jnp.concatenate(
        [one_hot(index_ref[pl.ds(c, 1), :], shard * PATCH_DEV) for c in range(rows // 128)],
        axis=1,
    )
    pooled = dot_nn(hot, grads[...])
    for load in loads[soon:]:
        load.wait()

    total[...] = pooled

    @pl.when(has_next)
    def _():
        for pair in range(pairs):
            prev_copies[pair].wait_recv()
            for n in range(2):
                total[:, pl.ds((n + 1) * width + pair * PAIR, PAIR)] += from_next[
                    pair, pl.ds(n * PATCH_DEV, PATCH_DEV), :
                ].astype(F32)
            total[pl.ds(PATCH_DEV - REACH, REACH), lanes(pair)] += from_next[
                pair, pl.ds(2 * PATCH_DEV, REACH), :
            ].astype(F32)

    def project(first):
        part = total[pl.ds(first, PATCH_DEV // 2), :].astype(BF16)
        return dot_nt(part, weights[...])

    side = PATCH_DEV // 2
    part = side // PARTS

    def swap(src, dst, sends, recvs, mate):
        return [
            pltpu.make_async_remote_copy(
                src_ref=src.at[pl.ds(n * part, part)],
                dst_ref=dst.at[pl.ds(n * part, part)],
                send_sem=sends.at[n],
                recv_sem=recvs.at[n],
                device_id=(shard, mate),
                device_id_type=MESH,
            )
            for n in range(PARTS)
        ]

    core_copies = swap(give, take, core_send, core_recv, near)
    far_copies = swap(half, half_in, far_send, far_recv, far)
    near_copies = swap(done, last, near_send, near_recv, near)
    give[...] = project(pl.multiple_of((1 - core) * side, side)).astype(BF16)
    for copy in core_copies:
        copy.start()
    kept[...] = project(pl.multiple_of(core * side, side))
    for n in range(PARTS):
        piece = pl.ds(n * part, part)
        core_copies[n].wait_recv()
        kept[piece, :] += take[piece, :].astype(F32)
        half[piece, :] = kept[piece, :].astype(BF16)
        far_copies[n].start()
    for n in range(PARTS):
        piece = pl.ds(n * part, part)
        far_copies[n].wait_recv()
        done[piece, :] = (kept[piece, :] + half_in[piece, :].astype(F32)).astype(BF16)
        near_copies[n].start()
    out_ref[pl.ds(pl.multiple_of(core * side, side), side), :] = dot_nn(
        done[...], unpatch[...]
    ).astype(BF16)
    for copy in near_copies:
        copy.wait_recv()
    out_ref[pl.ds(pl.multiple_of((1 - core) * side, side), side), :] = dot_nn(
        last[...], unpatch[...]
    ).astype(BF16)
    for copy in core_copies + far_copies + near_copies:
        copy.wait_send()

    @pl.when(has_prev)
    def _():
        for copy in prev_copies:
            copy.wait_send()

    @pl.when(has_next)
    def _():
        for copy in halos:
            copy.wait_send()


def on_device(
    shards,
    queries,
    byte_keys,
    byte_values,
    w_query,
    w_key,
    w_value,
    w_out,
    d_output,
    patch_index,
    unpatch,
):
    rows, width = queries.shape
    full = w_query.shape[0]
    out_width = unpatch.shape[1]
    pairs = width // PAIR
    side = PATCH_DEV // 2
    vmem = pltpu.VMEM
    dma = pltpu.SemaphoreType.DMA
    anywhere = pl.BlockSpec(memory_space=pl.ANY)
    local = pl.BlockSpec(memory_space=pltpu.VMEM)
    return pl.pallas_call(
        functools.partial(kernel, shards),
        out_shape=jax.ShapeDtypeStruct((PATCH_DEV, out_width), BF16),
        in_specs=[anywhere] * 8 + [local, anywhere],
        out_specs=local,
        scratch_shapes=[
            vmem((pairs, rows, PAIR), BF16),
            vmem((pairs, rows + WINDOW, PAIR), BF16),
            vmem((pairs, rows + WINDOW, PAIR), BF16),
            vmem((full, 3 * width), BF16),
            vmem(w_out.shape, BF16),
            vmem(d_output.shape, BF16),
            vmem(unpatch.shape, BF16),
            vmem((pairs, rows, PAIR), BF16),
            vmem((pairs, rows + WINDOW, PAIR), F32),
            vmem((pairs, rows + WINDOW, PAIR), F32),
            vmem((rows, 3 * width), BF16),
            vmem((2, SPAN, 2 * CHUNK), F32),
            vmem((2, SPAN, 2 * CHUNK), F32),
            vmem((SPAN + CHUNK, 4 * CHUNK), BF16),
            vmem((SPAN + CHUNK, 4 * CHUNK), BF16),
            vmem((8, 128), jnp.int32),
            vmem((pairs, 2 * PATCH_DEV + REACH, PAIR), BF16),
            vmem((pairs, 2 * PATCH_DEV + REACH, PAIR), BF16),
            vmem((side, full), BF16),
            vmem((side, full), BF16),
            vmem((side, full), BF16),
            vmem((side, full), BF16),
            vmem((side, full), BF16),
            vmem((side, full), BF16),
            vmem((side, full), F32),
            vmem((PATCH_DEV, 3 * width), F32),
            dma((5 + 5 * pairs + rows // BLOCK,)),
            dma((1 + 4 * pairs,)),
            dma((1 + 4 * pairs,)),
            dma((pairs,)),
            dma((pairs,)),
            dma((PARTS,)),
            dma((PARTS,)),
            dma((PARTS,)),
            dma((PARTS,)),
            dma((PARTS,)),
            dma((PARTS,)),
        ],
        compiler_params=pltpu.CompilerParams(
            collective_id=0, has_side_effects=True, vmem_limit_bytes=56 * 1024 * 1024
        ),
        name="fused_backward",
    )(
        queries,
        byte_keys,
        byte_values,
        w_query,
        w_key,
        w_value,
        w_out,
        d_output,
        patch_index.reshape(8, 128),
        unpatch,
    )


def solution(mesh):
    in_specs = (
        P("seq", "mp"),
        P("seq", "mp"),
        P("seq", "mp"),
        P(None, "mp"),
        P(None, "mp"),
        P(None, "mp"),
        P("mp", None),
        P("seq", None),
        P("seq"),
        P(None, "mp"),
    )
    return jax.shard_map(
        functools.partial(on_device, mesh.shape["seq"]),
        mesh=mesh,
        in_specs=in_specs,
        out_specs=P("seq", "mp"),
        check_vma=False,
    )
```

```python
import functools

import jax
import jax.numpy as jnp
from jax import lax
from jax.experimental import pallas as pl
from jax.experimental.pallas import tpu as pltpu
from jax.sharding import PartitionSpec as P

HS = 64
WINDOW = 512
PATCH_DEV = 256
BLOCK = 256
CHUNK = 128
SPAN = WINDOW + CHUNK
PAIR = 2 * HS
PARTS = 4
REACH = 128
PIECES = SPAN // CHUNK
MESH = pl.DeviceIdType.MESH
F32 = jnp.float32
BF16 = jnp.bfloat16


def dot_nt(a, b):
    return lax.dot_general(a, b, (((1,), (1,)), ((), ())), preferred_element_type=F32)


def dot_nn(a, b):
    return lax.dot_general(a, b, (((1,), (0,)), ((), ())), preferred_element_type=F32)


def kernel(
    shards,
    q_hbm,
    k_hbm,
    v_hbm,
    wq_hbm,
    wk_hbm,
    wv_hbm,
    wout_hbm,
    dout_hbm,
    index_ref,
    unpatch_hbm,
    out_ref,
    q,
    kx,
    vx,
    weights,
    wout,
    dout,
    unpatch,
    g,
    dk,
    dv,
    grads,
    scores,
    d_attend,
    p_low,
    ds_low,
    halo_index,
    prev,
    from_next,
    give,
    take,
    half,
    half_in,
    done,
    last,
    kept,
    total,
    load_sem,
    halo_send,
    halo_recv,
    prev_send,
    prev_recv,
    core_send,
    core_recv,
    far_send,
    far_recv,
    near_send,
    near_recv,
):
    rows = q_hbm.shape[0]
    width = q_hbm.shape[1]
    pairs = width // PAIR
    shard = lax.axis_index("seq")
    me = lax.axis_index("mp")
    core = lax.rem(me, 2)
    near = me + 1 - 2 * core
    far = lax.rem(me + 2, 4)
    has_prev = shard > 0
    has_next = shard < shards - 1

    def lanes(pair):
        return pl.ds(pair * PAIR, PAIR)

    own = pl.ds(WINDOW, rows)
    tail = rows - WINDOW
    moves = []
    for pair in range(pairs):
        for src, dst in ((k_hbm, kx), (v_hbm, vx)):
            moves.append((src.at[pl.ds(tail, WINDOW), lanes(pair)], dst.at[pair, pl.ds(rows, WINDOW)]))
    first_moves = len(moves)
    for pair in range(pairs):
        for src, dst in ((k_hbm, kx), (v_hbm, vx)):
            moves.append((src.at[pl.ds(0, tail), lanes(pair)], dst.at[pair, pl.ds(WINDOW, tail)]))
    moves.append((wout_hbm, wout))
    for pair in range(pairs):
        moves.append((q_hbm.at[:, lanes(pair)], q.at[pair]))
    output_moves = len(moves)
    for n in range(rows // BLOCK):
        mine = pl.ds(n * BLOCK, BLOCK)
        moves.append((dout_hbm.at[mine], dout.at[mine]))
    soon = len(moves)
    moves += [
        (src, weights.at[:, pl.ds(n * width, width)])
        for n, src in enumerate((wq_hbm, wk_hbm, wv_hbm))
    ]
    moves.append((unpatch_hbm, unpatch))
    loads = [
        pltpu.make_async_copy(src, dst, load_sem.at[n]) for n, (src, dst) in enumerate(moves)
    ]
    for load in loads[:soon]:
        load.start()

    barrier = pltpu.get_barrier_semaphore()
    for mate in (near, far):
        pl.semaphore_signal(barrier, inc=1, device_id=(shard, mate), device_id_type=MESH)

    @pl.when(has_prev)
    def _():
        pl.semaphore_signal(barrier, inc=1, device_id=(shard - 1, me), device_id_type=MESH)

    @pl.when(has_next)
    def _():
        pl.semaphore_signal(barrier, inc=1, device_id=(shard + 1, me), device_id_type=MESH)

    peers = 2 + has_prev.astype(jnp.int32) + has_next.astype(jnp.int32)
    pl.semaphore_wait(barrier, peers)

    def halo(n, src, dst):
        return pltpu.make_async_remote_copy(
            src_ref=src,
            dst_ref=dst,
            send_sem=halo_send.at[n],
            recv_sem=halo_recv.at[n],
            device_id=(shard + 1, me),
            device_id_type=MESH,
        )

    halos = [halo(0, index_ref, halo_index)]
    for pair in range(pairs):
        for first in (BLOCK, 0):
            for held in (kx, vx):
                halos.append(
                    halo(
                        len(halos),
                        held.at[pair, pl.ds(rows + first, BLOCK)],
                        held.at[pair, pl.ds(first, BLOCK)],
                    )
                )
    for load in loads[:first_moves]:
        load.wait()

    @pl.when(has_next)
    def _():
        for copy in halos[:5]:
            copy.start()

    @pl.when(shard == 0)
    def _():
        kx[:, pl.ds(0, WINDOW), :] = jnp.zeros((pairs, WINDOW, PAIR), BF16)
        vx[:, pl.ds(0, WINDOW), :] = jnp.zeros((pairs, WINDOW, PAIR), BF16)
        halo_index[...] = jnp.zeros_like(halo_index)

    dk[...] = jnp.zeros_like(dk)
    dv[...] = jnp.zeros_like(dv)
    for load in loads[first_moves:output_moves]:
        load.wait()

    for n in range(rows // BLOCK):
        loads[output_moves + n].wait()
        mine = pl.ds(n * BLOCK, BLOCK)
        heads_grad = dot_nt(dout[mine, :], wout[...]).astype(BF16)
        for pair in range(pairs):
            g[pair, mine, :] = heads_grad[:, pair * PAIR : (pair + 1) * PAIR]
    for load in loads[soon:]:
        load.start()

    def one_hot(index_row, base):
        slot = lax.broadcasted_iota(jnp.int32, (PATCH_DEV, 128), 0)
        return jnp.where(slot == index_row - base, 1.0, 0.0).astype(BF16)

    first_head = lax.broadcasted_iota(jnp.int32, (CHUNK, PAIR), 1) < HS

    def by_head(rows_of):
        blank = jnp.zeros_like(rows_of)
        return jnp.concatenate(
            [jnp.where(first_head, rows_of, blank), jnp.where(first_head, blank, rows_of)], axis=0
        )

    prev_copies = [
        pltpu.make_async_remote_copy(
            src_ref=prev.at[pair],
            dst_ref=from_next.at[pair],
            send_sem=prev_send.at[pair],
            recv_sem=prev_recv.at[pair],
            device_id=(shard - 1, me),
            device_id_type=MESH,
        )
        for pair in range(pairs)
    ]

    def send_prev(pair):
        base = (shard - 1) * PATCH_DEV
        hot = jnp.concatenate(
            [one_hot(halo_index[pl.ds(4 + c, 1), :], base) for c in range(WINDOW // 128)]
            + [one_hot(index_ref[pl.ds(0, 1), :], base)],
            axis=1,
        )
        span = pl.ds(0, WINDOW + 128)
        terms = jnp.concatenate([dk[pair, span, :], dv[pair, span, :]], axis=1).astype(BF16)
        terms = dot_nn(hot, terms).astype(BF16)
        prev[pair, pl.ds(0, PATCH_DEV), :] = terms[:, :PAIR]
        prev[pair, pl.ds(PATCH_DEV, PATCH_DEV), :] = terms[:, PAIR:]
        prev[pair, pl.ds(2 * PATCH_DEV, REACH), :] = dot_nn(
            hot[PATCH_DEV - REACH :, WINDOW:], grads[pl.ds(0, REACH), lanes(pair)]
        ).astype(BF16)
        prev_copies[pair].start()

    top_key = lax.broadcasted_iota(jnp.int32, (CHUNK, 2 * CHUNK), 0)
    query_pos = lax.rem(lax.broadcasted_iota(jnp.int32, (CHUNK, 2 * CHUNK), 1), CHUNK)

    def column(row):
        return jnp.broadcast_to(row, (PAIR, CHUNK)).T

    def one_step(step, carry):
        block = jnp.where(step < 2, 2, jnp.where(step < 6, 1 - lax.rem(step, 2), 3))
        pair = jnp.where((step >= 2) & (step < 6), (step - 2) // 2, lax.rem(step, 2))

        @pl.when((step == 2) & has_next)
        def _():
            for copy in halos[5:]:
                copy.start()

        for n in range(4):

            @pl.when((step == 2 + n) & has_prev)
            def _(n=n):
                if n == 0:
                    halos[0].wait_recv()
                halos[1 + 2 * n].wait_recv()
                halos[2 + 2 * n].wait_recv()

        for n in range(pairs):

            @pl.when((step == 4 + 2 * n) & has_prev)
            def _(n=n):
                send_prev(n)

        origin = pl.multiple_of(block * BLOCK, BLOCK)
        window = pl.ds(origin, WINDOW + BLOCK)
        keys_t = kx[pair, window, :].T
        scaled_q, scaled_g = [], []
        for c in range(BLOCK // CHUNK):
            start = pl.multiple_of(origin + c * CHUNK, CHUNK)
            mine = pl.ds(start, CHUNK)
            side_lanes = pl.ds(c * 2 * CHUNK, 2 * CHUNK)
            blocked = jnp.where(shard == 0, jnp.maximum(WINDOW - start, 0), 0)
            q_rows = q[pair, mine, :].astype(F32) * HS**-0.5
            g_rows = g[pair, mine, :]
            queries = by_head(q_rows.astype(BF16))
            grads_in = by_head(g_rows)
            raw = dot_nt(kx[pair, pl.ds(start, SPAN), :], queries)
            peak = None
            for n in range(PIECES):
                piece = pl.ds(n * CHUNK, CHUNK)
                part = raw[n * CHUNK : (n + 1) * CHUNK, :]
                if n == 0:
                    part = jnp.where(top_key > jnp.maximum(query_pos, blocked - 1), part, -1e30)
                elif n == PIECES - 1:
                    part = jnp.where(top_key <= query_pos, part, -1e30)
                else:
                    part = jnp.where(top_key >= blocked - n * CHUNK, part, -1e30)
                scores[c, piece, :] = part
                best = jnp.max(part.reshape(CHUNK // 8, 8, 2 * CHUNK), axis=0)
                peak = best if peak is None else jnp.maximum(peak, best)
            peak = jnp.max(peak, axis=0, keepdims=True)
            weight = jnp.zeros((8, 2 * CHUNK), F32)
            mixed = jnp.zeros((8, 2 * CHUNK), F32)
            raw = dot_nt(vx[pair, pl.ds(start, SPAN), :], grads_in)
            for n in range(PIECES):
                piece = pl.ds(n * CHUNK, CHUNK)
                raised = jnp.exp(scores[c, piece, :] - peak)
                part = raw[n * CHUNK : (n + 1) * CHUNK, :]
                d_attend[c, piece, :] = part
                p_low[pl.ds((c + n) * CHUNK, CHUNK), side_lanes] = raised.astype(BF16)
                weight += jnp.sum(raised.reshape(CHUNK // 8, 8, 2 * CHUNK), axis=0)
                mixed += jnp.sum((raised * part).reshape(CHUNK // 8, 8, 2 * CHUNK), axis=0)
            inverse = 1.0 / jnp.sum(weight, axis=0, keepdims=True)
            row_dot = jnp.sum(mixed, axis=0, keepdims=True) * inverse
            for n in range(PIECES):
                piece = pl.ds(n * CHUNK, CHUNK)
                place = pl.ds((c + n) * CHUNK, CHUNK)
                ds_low[place, side_lanes] = (
                    p_low[place, side_lanes].astype(F32) * (d_attend[c, piece, :] - row_dot)
                ).astype(BF16)
            scale = jnp.where(
                first_head, column(inverse[:, :CHUNK]), column(inverse[:, CHUNK:])
            )
            scaled_q.append(by_head((q_rows * scale).astype(BF16)))
            scaled_g.append(by_head((g_rows.astype(F32) * scale).astype(BF16)))
            d_query = dot_nn(
                keys_t[:, c * CHUNK : c * CHUNK + SPAN],
                ds_low[pl.ds(c * CHUNK, SPAN), side_lanes],
            ) * (inverse * HS**-0.5)
            d_query = jnp.concatenate([d_query[:HS, :CHUNK], d_query[HS:, CHUNK:]], axis=0)
            grads[mine, pl.ds(pl.multiple_of(pair * PAIR, PAIR), PAIR)] = d_query.T.astype(BF16)
        for held, low, rows_of in ((dk, ds_low, scaled_q), (dv, p_low, scaled_g)):
            held[pair, pl.ds(origin, CHUNK), :] += dot_nn(
                low[pl.ds(0, CHUNK), pl.ds(0, 2 * CHUNK)], rows_of[0]
            )
            held[pair, pl.ds(origin + CHUNK, WINDOW), :] += dot_nn(
                low[pl.ds(CHUNK, WINDOW), :], jnp.concatenate(rows_of, axis=0)
            )
            held[pair, pl.ds(origin + SPAN, CHUNK), :] += dot_nn(
                low[pl.ds(SPAN, CHUNK), pl.ds(2 * CHUNK, 2 * CHUNK)], rows_of[1]
            )
        return carry

    lax.fori_loop(0, rows // BLOCK * pairs, one_step, 0)

    for pair in range(pairs):
        grads[:, pl.ds(width + pair * PAIR, PAIR)] = dk[pair, own, :].astype(BF16)
        grads[:, pl.ds(2 * width + pair * PAIR, PAIR)] = dv[pair, own, :].astype(BF16)
    hot = jnp.concatenate(
        [one_hot(index_ref[pl.ds(c, 1), :], shard * PATCH_DEV) for c in range(rows // 128)],
        axis=1,
    )
    pooled = dot_nn(hot, grads[...])
    for load in loads[soon:]:
        load.wait()

    total[...] = pooled

    @pl.when(has_next)
    def _():
        for pair in range(pairs):
            prev_copies[pair].wait_recv()
            for n in range(2):
                total[:, pl.ds((n + 1) * width + pair * PAIR, PAIR)] += from_next[
                    pair, pl.ds(n * PATCH_DEV, PATCH_DEV), :
                ].astype(F32)
            total[pl.ds(PATCH_DEV - REACH, REACH), lanes(pair)] += from_next[
                pair, pl.ds(2 * PATCH_DEV, REACH), :
            ].astype(F32)

    def project(first):
        part = total[pl.ds(first, PATCH_DEV // 2), :].astype(BF16)
        return dot_nt(part, weights[...])

    side = PATCH_DEV // 2
    part = side // PARTS

    def swap(src, dst, sends, recvs, mate):
        return [
            pltpu.make_async_remote_copy(
                src_ref=src.at[pl.ds(n * part, part)],
                dst_ref=dst.at[pl.ds(n * part, part)],
                send_sem=sends.at[n],
                recv_sem=recvs.at[n],
                device_id=(shard, mate),
                device_id_type=MESH,
            )
            for n in range(PARTS)
        ]

    core_copies = swap(give, take, core_send, core_recv, near)
    far_copies = swap(half, half_in, far_send, far_recv, far)
    near_copies = swap(done, last, near_send, near_recv, near)
    give[...] = project(pl.multiple_of((1 - core) * side, side)).astype(BF16)
    for copy in core_copies:
        copy.start()
    kept[...] = project(pl.multiple_of(core * side, side))
    for n in range(PARTS):
        piece = pl.ds(n * part, part)
        core_copies[n].wait_recv()
        kept[piece, :] += take[piece, :].astype(F32)
        half[piece, :] = kept[piece, :].astype(BF16)
        far_copies[n].start()
    for n in range(PARTS):
        piece = pl.ds(n * part, part)
        far_copies[n].wait_recv()
        done[piece, :] = (kept[piece, :] + half_in[piece, :].astype(F32)).astype(BF16)
        near_copies[n].start()
    out_ref[pl.ds(pl.multiple_of(core * side, side), side), :] = dot_nn(
        done[...], unpatch[...]
    ).astype(BF16)
    for copy in near_copies:
        copy.wait_recv()
    out_ref[pl.ds(pl.multiple_of((1 - core) * side, side), side), :] = dot_nn(
        last[...], unpatch[...]
    ).astype(BF16)
    for copy in core_copies + far_copies + near_copies:
        copy.wait_send()

    @pl.when(has_prev)
    def _():
        for copy in prev_copies:
            copy.wait_send()

    @pl.when(has_next)
    def _():
        for copy in halos:
            copy.wait_send()


def on_device(
    shards,
    queries,
    byte_keys,
    byte_values,
    w_query,
    w_key,
    w_value,
    w_out,
    d_output,
    patch_index,
    unpatch,
):
    rows, width = queries.shape
    full = w_query.shape[0]
    out_width = unpatch.shape[1]
    pairs = width // PAIR
    side = PATCH_DEV // 2
    vmem = pltpu.VMEM
    dma = pltpu.SemaphoreType.DMA
    anywhere = pl.BlockSpec(memory_space=pl.ANY)
    local = pl.BlockSpec(memory_space=pltpu.VMEM)
    return pl.pallas_call(
        functools.partial(kernel, shards),
        out_shape=jax.ShapeDtypeStruct((PATCH_DEV, out_width), BF16),
        in_specs=[anywhere] * 8 + [local, anywhere],
        out_specs=local,
        scratch_shapes=[
            vmem((pairs, rows, PAIR), BF16),
            vmem((pairs, rows + WINDOW, PAIR), BF16),
            vmem((pairs, rows + WINDOW, PAIR), BF16),
            vmem((full, 3 * width), BF16),
            vmem(w_out.shape, BF16),
            vmem(d_output.shape, BF16),
            vmem(unpatch.shape, BF16),
            vmem((pairs, rows, PAIR), BF16),
            vmem((pairs, rows + WINDOW, PAIR), F32),
            vmem((pairs, rows + WINDOW, PAIR), F32),
            vmem((rows, 3 * width), BF16),
            vmem((2, SPAN, 2 * CHUNK), F32),
            vmem((2, SPAN, 2 * CHUNK), F32),
            vmem((SPAN + CHUNK, 4 * CHUNK), BF16),
            vmem((SPAN + CHUNK, 4 * CHUNK), BF16),
            vmem((8, 128), jnp.int32),
            vmem((pairs, 2 * PATCH_DEV + REACH, PAIR), BF16),
            vmem((pairs, 2 * PATCH_DEV + REACH, PAIR), BF16),
            vmem((side, full), BF16),
            vmem((side, full), BF16),
            vmem((side, full), BF16),
            vmem((side, full), BF16),
            vmem((side, full), BF16),
            vmem((side, full), BF16),
            vmem((side, full), F32),
            vmem((PATCH_DEV, 3 * width), F32),
            dma((5 + 5 * pairs + rows // BLOCK,)),
            dma((1 + 4 * pairs,)),
            dma((1 + 4 * pairs,)),
            dma((pairs,)),
            dma((pairs,)),
            dma((PARTS,)),
            dma((PARTS,)),
            dma((PARTS,)),
            dma((PARTS,)),
            dma((PARTS,)),
            dma((PARTS,)),
        ],
        compiler_params=pltpu.CompilerParams(
            collective_id=0, has_side_effects=True, vmem_limit_bytes=56 * 1024 * 1024
        ),
        name="fused_backward",
    )(
        queries,
        byte_keys,
        byte_values,
        w_query,
        w_key,
        w_value,
        w_out,
        d_output,
        patch_index.reshape(8, 128),
        unpatch,
    )


def solution(mesh):
    in_specs = (
        P("seq", "mp"),
        P("seq", "mp"),
        P("seq", "mp"),
        P(None, "mp"),
        P(None, "mp"),
        P(None, "mp"),
        P("mp", None),
        P("seq", None),
        P("seq"),
        P(None, "mp"),
    )
    return jax.shard_map(
        functools.partial(on_device, mesh.shape["seq"]),
        mesh=mesh,
        in_specs=in_specs,
        out_specs=P("seq", "mp"),
        check_vma=False,
    )
```
